128 devices in a mesh: pipe: 8 (over x, core), ctx: 16 (over y, z).
Axes of the slice: x: 4, y: 4, z: 4, core: 2. Of those that a mesh axis runs over, the one named last changes fastest.
Arguments:
- key_blocks: int32 [1, 16, 3], replicated, may hold values from -1 to 15, as said below
- ranker: int32 [1, 2048], replicated, may hold values from 0 to 1
- section_inputs: bfloat16 [8, 1, 2048, 1024], P('pipe', None, 'ctx'), may hold values from -6 to 6
- output_grad: bfloat16 [1, 2048, 1024], P(None, 'ctx'), may hold values from -6 to 6
- input_proj: bfloat16 [8, 4096, 1024], P('pipe'), may hold values from -0.1875 to 0.1875
- output_proj: bfloat16 [8, 1024, 1024], P('pipe'), may hold values from -0.1875 to 0.1875
- norm_gain: float32 [8, 1024], P('pipe'), may hold values from 0.5 to 1.5
Outputs:
- section_grads: bfloat16 [8, 1, 2048, 1024], P('pipe', None, 'ctx')
- input_proj_grad: float32 [8, 4096, 1024], P('pipe', 'ctx')
The draws below stay inside these ranges and needn't reach their ends.
Inputs may be any that keep to these rules, and one draw needn't show every extreme that they name: `key_blocks`: row n of history h: slot 0 is n, slot 1 is n - 1, the next slots are distinct earlier blocks; -1 marks unused slots and only follows the used ones. Lists hold 2 to 3 used slots, fewer near the start.
All inputs are finite; a program needn't handle non-finite values.
Results may differ from the reference program's by a relative error of at most 0.034.
Values may be sent and summed in bfloat16 or wider, within the bound.
A program may use at most 128 MiB of HBM per device.

```python
import jax
import jax.numpy as jnp
from jax import lax

D = 1024
H = 16
BLOCK = 128
KB = 3
SEQS = 1
SECTIONS = 8
LEN = 2048
NQB = 16


def draw_key_blocks(key, part):
    key = jax.random.fold_in(key, 17)
    pick_key, count_key = jax.random.split(key)
    own_block = jnp.arange(NQB, dtype=jnp.int32)[None, :, None]
    spans = jnp.arange(2, NQB, dtype=jnp.int32)[None, None, :]
    random_scores = jax.random.randint(pick_key, (SEQS, NQB, NQB - 2), 0, 1 << 20, dtype=jnp.int32)
    ranked = jnp.where(spans <= own_block, random_scores * NQB + spans, -spans)
    chosen, _ = lax.top_k(ranked, KB - 2)
    distances = chosen % NQB
    earlier = jnp.where(chosen >= 0, own_block - distances, -1)
    previous = jnp.where(own_block >= 1, own_block - 1, -1)
    lists = jnp.concatenate([jnp.broadcast_to(own_block, (SEQS, NQB, 1)), jnp.broadcast_to(previous, (SEQS, NQB, 1)), earlier], axis=2)
    used = jax.random.randint(count_key, (SEQS, NQB, 1), 2, KB + 1, dtype=jnp.int32)
    slots = jnp.arange(KB, dtype=jnp.int32)[None, None, :]
    return jnp.where(slots < used, lists, -1).astype(jnp.int32)


def touch_ends(drawn, own_key, least, high):
    index_at = [jax.random.randint(jax.random.fold_in(own_key, axis), (), 0, length) for axis, length in enumerate(drawn.shape)]
    main_axis = drawn.shape.index(max(drawn.shape))
    beside = index_at[:main_axis] + [(index_at[main_axis] + 1) % drawn.shape[main_axis]] + index_at[main_axis + 1:]
    return drawn.at[tuple(index_at)].set(least).at[tuple(beside)].set(high)


def shard_levels(own_key, shape, shards, least, top_value):
    def one(axis_at, blocks):
        draws = jax.random.uniform(jax.random.fold_in(jax.random.fold_in(own_key, 6), axis_at), (blocks,), jnp.float32, least / len(shards), top_value / len(shards))
        return jnp.repeat(jnp.exp(draws), shape[axis_at] // blocks).reshape((-1,) + (1,) * (len(shape) - axis_at - 1))

    level = one(*shards[0])
    for cut in shards[1:]:
        level = level * one(*cut)
    return level


def bell_draw(own_key, extent, deviation, bound, shards=(), kind=jnp.bfloat16):
    array = deviation * jax.random.normal(own_key, extent, jnp.float32)
    if shards:
        array = array * shard_levels(own_key, extent, shards, -0.22, 0.18)
    return jnp.clip(array, -bound, bound).astype(kind)


def setup_inputs(seed: int = 0) -> dict:
    keys = jax.random.split(jax.random.key(seed), 8)
    return {
        "key_blocks": draw_key_blocks(jax.random.fold_in(keys[7], 71), 0),
        "ranker": touch_ends(jax.random.randint(keys[1], (SEQS, LEN), 0, 2), jax.random.fold_in(keys[1], 1), 0, 1).astype(jnp.int32),
        "section_inputs": bell_draw(keys[2], (SECTIONS, SEQS, LEN, D), 1.0, 6.0, ((0, 8), (2, 16))),
        "output_grad": bell_draw(keys[3], (SEQS, LEN, D), 1.0, 6.0, ((1, 16),)),
        "input_proj": bell_draw(keys[4], (SECTIONS, 4 * D, D), D ** -0.5, 0.1875, ((0, 8),)),
        "output_proj": bell_draw(keys[5], (SECTIONS, D, D), D ** -0.5, 0.1875, ((0, 8),)),
        "norm_gain": jnp.clip(1.0 + 0.1 * jax.random.normal(keys[6], (SECTIONS, D), jnp.float32), 0.5, 1.5),
    }


def silu_slope(argument):
    sigma = jax.nn.sigmoid(argument)
    return sigma * (1.0 + argument * (1.0 - sigma))

def build_allowed(blocks, rankers, block_count):
    length = block_count * BLOCK
    offsets = jnp.arange(BLOCK, dtype=jnp.int32)
    key_pos = blocks[:, :, None] * BLOCK + offsets[None, None, :]
    query_pos = jnp.arange(length, dtype=jnp.int32).reshape(block_count, BLOCK)
    safe_pos = jnp.clip(key_pos, 0, length - 1)
    key_rank = rankers[safe_pos]
    query_rank = rankers.reshape(block_count, BLOCK)
    live = (blocks >= 0)[:, None, :, None]
    causal = key_pos[:, None, :, :] <= query_pos[:, :, None, None]
    same_rank = key_rank[:, None, :, :] == query_rank[:, :, None, None]
    return live & causal & same_rank

def head_backward(projected, cot_gate, gain_heads, blocks, rankers):
    head_count, _, head_width, length = projected.shape
    block_count = length // BLOCK
    score_scale = head_width ** (-0.5)
    pre_float = projected.astype(jnp.float32)
    activated = jax.nn.silu(pre_float).astype(jnp.bfloat16)
    gate_act = activated[:, 0]
    value_act = activated[:, 1]
    query_act = activated[:, 2].reshape(head_count, head_width, block_count, BLOCK)
    key_act = activated[:, 3].reshape(head_count, head_width, block_count, BLOCK)
    select = (blocks[:, :, None] == jnp.arange(block_count, dtype=jnp.int32)[None, None, :]).astype(jnp.float32)
    key_tiles = jnp.einsum('hdmc,nkm->hdnkc', key_act.astype(jnp.float32), select).astype(jnp.bfloat16)
    value_tiles = jnp.einsum('hdmc,nkm->hdnkc', value_act.reshape(head_count, head_width, block_count, BLOCK).astype(jnp.float32), select).astype(jnp.bfloat16)
    allowed = build_allowed(blocks, rankers, block_count)[None]
    scores = jnp.einsum('hdnq,hdnkc->hnqkc', query_act.astype(jnp.float32), key_tiles.astype(jnp.float32)) * score_scale
    weights = jnp.where(allowed, jax.nn.silu(scores), 0.0).astype(jnp.bfloat16)
    attended = jnp.einsum('hnqkc,hdnkc->hdnq', weights.astype(jnp.float32), value_tiles.astype(jnp.float32)).reshape(head_count, head_width, length)
    inv_rms = lax.rsqrt(lax.optimization_barrier(jnp.mean(attended * attended, axis=1, keepdims=True)) + 1.0)
    normed = attended * inv_rms
    scaled = cot_gate.astype(jnp.float32) * gain_heads[:, :, None]
    grad_gate = scaled * normed
    grad_normed = scaled * gate_act.astype(jnp.float32)
    grad_attended = (inv_rms * (grad_normed - normed * lax.optimization_barrier(jnp.mean(grad_normed * normed, axis=1, keepdims=True)))).astype(jnp.bfloat16)
    grad_attended = grad_attended.reshape(head_count, head_width, block_count, BLOCK).astype(jnp.float32)
    grad_weights = jnp.einsum('hdnq,hdnkc->hnqkc', grad_attended, value_tiles.astype(jnp.float32))
    value_tile_grads = jnp.einsum('hnqkc,hdnq->hdnkc', weights.astype(jnp.float32), grad_attended)
    grad_value = jnp.einsum('hdnkc,nkm->hdmc', value_tile_grads, select).reshape(head_count, head_width, length)
    grad_scores = (grad_weights * jnp.where(allowed, silu_slope(scores), 0.0) * score_scale).astype(jnp.bfloat16).astype(jnp.float32)
    grad_query = jnp.einsum('hnqkc,hdnkc->hdnq', grad_scores, key_tiles.astype(jnp.float32)).reshape(head_count, head_width, length)
    key_tile_grads = jnp.einsum('hnqkc,hdnq->hdnkc', grad_scores, query_act.astype(jnp.float32))
    grad_key = jnp.einsum('hdnkc,nkm->hdmc', key_tile_grads, select).reshape(head_count, head_width, length)
    grad_parts = jnp.stack([grad_gate, grad_value, grad_query, grad_key], axis=1)
    return (grad_parts * silu_slope(pre_float)).astype(jnp.bfloat16)

def reference(key_blocks, ranker, section_inputs, output_grad, input_proj, output_proj, norm_gain):
    section_total, seq_count, length, width_all = section_inputs.shape
    head_width = width_all // H
    norm_factor = float(seq_count * length) ** (-0.5)
    upstream_all = [output_grad[history] for history in range(seq_count)]
    grads_per_section = [None] * section_total
    weight_grads = [None] * section_total
    for section_pos in range(section_total - 1, -1, -1):
        summed = jnp.zeros((4 * width_all, width_all), jnp.float32)
        outgoing = []
        for history in range(seq_count):
            inputs_now = section_inputs[section_pos, history]
            upstream = upstream_all[history]
            projected = jnp.dot(input_proj[section_pos], inputs_now.T, preferred_element_type=jnp.float32).astype(jnp.bfloat16)
            projected = projected.reshape(H, 4, head_width, length)
            cot_gate = jnp.dot(upstream, output_proj[section_pos], preferred_element_type=jnp.float32).astype(jnp.bfloat16)
            cot_gate = cot_gate.T.reshape(H, head_width, length)
            gain_heads = norm_gain[section_pos].reshape(H, head_width)
            grad_heads = head_backward(projected, cot_gate, gain_heads, key_blocks[history], ranker[history])
            grad_rows = grad_heads.reshape(4 * width_all, length)
            section_grad = (upstream.astype(jnp.float32) + jnp.dot(grad_rows.T, input_proj[section_pos], preferred_element_type=jnp.float32)).astype(jnp.bfloat16)
            summed = summed + jnp.dot(grad_rows, inputs_now, preferred_element_type=jnp.float32)
            outgoing.append(section_grad)
        upstream_all = outgoing
        grads_per_section[section_pos] = jnp.stack(outgoing)
        weight_grads[section_pos] = summed * norm_factor
    return (jnp.stack(grads_per_section), jnp.stack(weight_grads))
```

```python
import functools

import jax
import jax.numpy as jnp
from jax import lax
from jax.experimental import pallas as pl
from jax.experimental.pallas import tpu as pltpu
from jax.sharding import PartitionSpec as P

BLOCK = 128
HD = 64
HOPS = 4
MESH = pl.DeviceIdType.MESH
F32 = jnp.float32
BF16 = jnp.bfloat16


def silu_slope(argument):
    sigma = jax.nn.sigmoid(argument)
    return sigma * (1.0 + argument * (1.0 - sigma))


def forward(proj, gain, blocks, ranker):
    count = proj.shape[0]
    scale = HD ** (-0.5)
    pre = proj.reshape(count, 4, HD, BLOCK).astype(F32)
    act = jax.nn.silu(pre).astype(BF16)
    slopes = silu_slope(pre)
    onehot = (blocks[:, :, None] == jnp.arange(count, dtype=jnp.int32)[None, None, :])
    half = onehot.astype(BF16)
    ktile = jnp.einsum("nsm,mjk->njsk", half, act[:, 3], preferred_element_type=F32).astype(BF16)
    vtile = jnp.einsum("nsm,mjk->nskj", half, act[:, 1], preferred_element_type=F32).astype(BF16)
    offsets = jnp.arange(BLOCK, dtype=jnp.int32)
    ranks = ranker.reshape(count, BLOCK).astype(F32)
    key_rank = jnp.einsum("nsm,mk->nsk", onehot.astype(F32), ranks)
    key_pos = blocks[:, :, None] * BLOCK + offsets
    query_pos = jnp.arange(count * BLOCK, dtype=jnp.int32).reshape(count, BLOCK)
    allowed = (
        (blocks >= 0)[:, :, None, None]
        & (key_pos[:, :, :, None] <= query_pos[:, None, None, :])
        & (key_rank[:, :, :, None] == ranks[:, None, None, :])
    )
    query = act[:, 2]
    scores = jnp.einsum("njsk,njq->nskq", ktile, query, preferred_element_type=F32) * scale
    weights = jnp.where(allowed, jax.nn.silu(scores), 0.0).astype(BF16)
    slope = (jnp.where(allowed, silu_slope(scores), 0.0) * scale).astype(BF16)
    attended = jnp.einsum("nskq,nskj->njq", weights, vtile, preferred_element_type=F32)
    inv_rms = lax.rsqrt(jnp.mean(attended * attended, axis=1, keepdims=True) + 1.0)
    normed = attended * inv_rms
    gain_col = gain[None, :, None]
    ahead = inv_rms * gain_col * act[:, 0].astype(F32)
    factors = jnp.stack([gain_col * normed * slopes[:, 0], slopes[:, 2], slopes[:, 1], slopes[:, 3]], axis=1)
    slots = blocks.shape[1]
    return (
        weights.reshape(count, slots * BLOCK, BLOCK),
        slope.reshape(count, slots * BLOCK, BLOCK),
        ktile.reshape(count, HD, slots * BLOCK),
        vtile.reshape(count, slots * BLOCK, HD),
        query,
        ahead,
        normed,
        factors,
    )


def segment_plan(third):
    count = third.shape[0]
    ids = jnp.arange(count, dtype=jnp.int32)
    before = (third[None, :] < third[:, None]) | ((third[None, :] == third[:, None]) & (ids[None, :] < ids[:, None]))
    place = jnp.sum(before.astype(jnp.int32), axis=1)
    order = jnp.sum(jnp.where(place[None, :] == ids[:, None], ids[None, :], 0), axis=1)
    ordered = jnp.sum(jnp.where(place[None, :] == ids[:, None], third[None, :], 0), axis=1)
    keep = (ordered == jnp.concatenate([ordered[:1] - 1, ordered[:-1]])).astype(F32)
    upto = jnp.sum((third[None, :] <= ids[:, None]).astype(jnp.int32), axis=1)
    has = jnp.any(third[None, :] == ids[:, None], axis=1).astype(F32)
    last = jnp.maximum(upto - 1, 0)
    return jnp.stack([order, last]), jnp.stack([keep, has])


def chain_kernel(
    order_ref, keep_ref, up_ref, wo_ref, wi_ref, w_ref, sp_ref, kt_ref, vt_ref, q_ref, ahead_ref, normed_ref, fac_ref,
    sg_ref, gpa_ref, gpb_ref,
    wot, upbuf, sgsend, cotsend, cotin, gain_a, gain_b, gvt, gkt, segv, segk, acc,
    cs, cr, as_, ar, bs, br, hs, hr,
):
    count = w_ref.shape[0]
    s = lax.axis_index("pipe")
    c = lax.axis_index("ctx")
    sections = lax.axis_size("pipe")
    width = up_ref.shape[1]
    cols = width // HOPS
    first = s == sections - 1

    def peer(d):
        return lax.rem(c + d, count)

    def behind(d):
        return lax.rem(c - d + count, count)

    barrier = pltpu.get_barrier_semaphore()
    for d in range(1, count):
        pl.semaphore_signal(barrier, inc=1, device_id=(s, peer(d)), device_id_type=MESH)

    for d in (1, sections - 1):
        pl.semaphore_signal(barrier, inc=1, device_id=(lax.rem(s + d, sections), c), device_id_type=MESH)

    wot[...] = wo_ref[...].T
    pl.semaphore_wait(barrier, count + 1)

    def hop(i):
        return pltpu.make_async_remote_copy(
            src_ref=sgsend.at[i], dst_ref=upbuf.at[i], send_sem=hs.at[i], recv_sem=hr.at[i],
            device_id=(s - 1, c), device_id_type=MESH,
        )

    @pl.when(first)
    def _():
        for i in range(HOPS):
            upbuf[i] = up_ref[:, i * cols : (i + 1) * cols]

    cot = None
    for i in range(HOPS):
        @pl.when(jnp.logical_not(first))
        def _(i=i):
            hop(i).wait_recv()

        part = lax.dot_general(
            wot[:, i * cols : (i + 1) * cols], upbuf[i], (((1,), (1,)), ((), ())), preferred_element_type=F32
        )
        cot = part if cot is None else cot + part
    cotsend[...] = cot.astype(BF16).reshape(count, HD, BLOCK)

    def cot_copy(d):
        h = peer(d)
        return pltpu.make_async_remote_copy(
            src_ref=cotsend.at[h], dst_ref=cotin.at[c], send_sem=cs.at[h], recv_sem=cr.at[c],
            device_id=(s, h), device_id_type=MESH,
        )

    def cot_arrival(n):
        return pltpu.make_async_remote_copy(
            src_ref=cotsend.at[n], dst_ref=cotin.at[n], send_sem=cs.at[n], recv_sem=cr.at[n],
            device_id=(s, n), device_id_type=MESH,
        )

    def start_cot(d, carry):
        cot_copy(d).start()
        return carry

    lax.fori_loop(1, count, start_cot, 0)
    cotin[c] = cotsend[c]

    def back_copy(src, landing, send, recv, n):
        return pltpu.make_async_remote_copy(
            src_ref=src.at[n], dst_ref=landing.at[c], send_sem=send.at[n], recv_sem=recv.at[c],
            device_id=(s, n), device_id_type=MESH,
        )

    def back_arrival(src, landing, send, recv, h):
        return pltpu.make_async_remote_copy(
            src_ref=src.at[h], dst_ref=landing.at[h], send_sem=send.at[h], recv_sem=recv.at[h],
            device_id=(s, h), device_id_type=MESH,
        )

    def head_step(i, carry):
        n = behind(i)

        @pl.when(i > 0)
        def _():
            cot_arrival(n).wait_recv()

        cot_n = cotin[n].astype(F32)
        normed = normed_ref[n]
        steep = cot_n * ahead_ref[n]
        mean = jnp.sum(steep * normed, axis=0, keepdims=True) * (1.0 / HD)
        ga = (steep - normed * mean).astype(BF16)
        gw = jnp.dot(vt_ref[n], ga, preferred_element_type=F32)
        gs = (gw * sp_ref[n].astype(F32)).astype(BF16)
        gq = jnp.dot(kt_ref[n], gs, preferred_element_type=F32)
        gpa_ref[n, :HD] = (cot_n * fac_ref[n, 0]).astype(BF16)
        gpa_ref[n, HD:] = (gq * fac_ref[n, 1]).astype(BF16)

        @pl.when(i > 0)
        def _():
            back_copy(gpa_ref, gain_a, as_, ar, n).start()

        gvt[n] = lax.dot_general(ga, w_ref[n], (((1,), (1,)), ((), ())), preferred_element_type=F32)
        gkt[n] = lax.dot_general(q_ref[n], gs, (((1,), (1,)), ((), ())), preferred_element_type=F32)
        return carry

    lax.fori_loop(0, count, head_step, 0)
    gain_a[c] = gpa_ref[c]

    def seg_step(i, carry):
        run_v, run_k = carry
        n = order_ref[0, i]
        keep = keep_ref[0, i]
        run_v = run_v * keep + gvt[n, :, 2 * BLOCK :]
        run_k = run_k * keep + gkt[n, :, 2 * BLOCK :]
        segv[i] = run_v
        segk[i] = run_k
        return run_v, run_k

    zero = jnp.zeros((HD, BLOCK), F32)
    lax.fori_loop(0, count, seg_step, (zero, zero))

    def final_step(i, carry):
        m = behind(i)
        after = lax.rem(m + 1, count)
        last = order_ref[1, m]
        has = keep_ref[1, m]
        gv = gvt[m, :, :BLOCK] + gvt[after, :, BLOCK : 2 * BLOCK] + segv[last] * has
        gk = gkt[m, :, :BLOCK] + gkt[after, :, BLOCK : 2 * BLOCK] + segk[last] * has
        gpb_ref[m, :HD] = (gv * fac_ref[m, 2]).astype(BF16)
        gpb_ref[m, HD:] = (gk * fac_ref[m, 3]).astype(BF16)

        @pl.when(i > 0)
        def _():
            back_copy(gpb_ref, gain_b, bs, br, m).start()

        return carry

    lax.fori_loop(0, count, final_step, 0)
    gain_b[c] = gpb_ref[c]

    for i in range(HOPS):
        acc[:, i * cols : (i + 1) * cols] = upbuf[i].astype(F32)

    def a_rows(h):
        return jnp.concatenate([wi_ref[h, 0], wi_ref[h, 2]], axis=0)

    def b_rows(h):
        return jnp.concatenate([wi_ref[h, 1], wi_ref[h, 3]], axis=0)

    def tdot(left, right):
        return lax.dot_general(left, right, (((0,), (0,)), ((), ())), preferred_element_type=F32)

    def a_step(i, carry):
        h0 = peer(2 * i)
        h1 = peer(2 * i + 1)

        @pl.when(i > 0)
        def _():
            back_arrival(gpa_ref, gain_a, as_, ar, h0).wait_recv()

        back_arrival(gpa_ref, gain_a, as_, ar, h1).wait_recv()
        left = jnp.concatenate([gain_a[h0], gain_a[h1]], axis=0)
        right = jnp.concatenate([a_rows(h0), a_rows(h1)], axis=0)
        acc[...] += tdot(left, right)
        return carry

    lax.fori_loop(0, count // 2, a_step, 0)

    def b_step(i, carry):
        h0 = peer(2 * i)
        h1 = peer(2 * i + 1)

        @pl.when(i > 0)
        def _():
            back_arrival(gpb_ref, gain_b, bs, br, h0).wait_recv()

        back_arrival(gpb_ref, gain_b, bs, br, h1).wait_recv()
        left = jnp.concatenate([gain_b[h0], gain_b[h1]], axis=0)
        right = jnp.concatenate([b_rows(h0), b_rows(h1)], axis=0)
        acc[...] += tdot(left, right)
        return carry

    lax.fori_loop(0, count // 2 - 1, b_step, 0)
    h0 = peer(count - 2)
    h1 = peer(count - 1)
    back_arrival(gpb_ref, gain_b, bs, br, h0).wait_recv()
    back_arrival(gpb_ref, gain_b, bs, br, h1).wait_recv()
    left = jnp.concatenate([gain_b[h0], gain_b[h1]], axis=0)
    for i in range(HOPS):
        span = slice(i * cols, (i + 1) * cols)
        right = jnp.concatenate(
            [wi_ref[h0, 1, :, span], wi_ref[h0, 3, :, span], wi_ref[h1, 1, :, span], wi_ref[h1, 3, :, span]], axis=0
        )
        part = (acc[:, span] + tdot(left, right)).astype(BF16)
        sgsend[i] = part

        @pl.when(s > 0)
        def _(i=i):
            hop(i).start()

        sg_ref[:, span] = part

    def finish(d, carry):
        h = peer(d)
        cot_copy(d).wait_send()
        back_copy(gpa_ref, gain_a, as_, ar, h).wait_send()
        back_copy(gpb_ref, gain_b, bs, br, h).wait_send()
        return carry

    lax.fori_loop(1, count, finish, 0)

    @pl.when(s > 0)
    def _():
        for i in range(HOPS):
            hop(i).wait_send()


def run_chain(plan, keep, up, wo, wi, fwd):
    count = fwd[0].shape[0]
    width = up.shape[1]
    vmem = pl.BlockSpec(memory_space=pltpu.VMEM)
    smem = pl.BlockSpec(memory_space=pltpu.SMEM)
    dma = pltpu.SemaphoreType.DMA
    slots = fwd[0].shape[1]
    pair = (count, 2 * HD, BLOCK)
    return pl.pallas_call(
        chain_kernel,
        out_shape=(
            jax.ShapeDtypeStruct((BLOCK, width), BF16),
            jax.ShapeDtypeStruct(pair, BF16),
            jax.ShapeDtypeStruct(pair, BF16),
        ),
        in_specs=[smem, smem] + [vmem] * 11,
        out_specs=(vmem, vmem, vmem),
        scratch_shapes=[
            pltpu.VMEM((width, width), BF16),
            pltpu.VMEM((HOPS, BLOCK, width // HOPS), BF16),
            pltpu.VMEM((HOPS, BLOCK, width // HOPS), BF16),
            pltpu.VMEM((count, HD, BLOCK), BF16),
            pltpu.VMEM((count, HD, BLOCK), BF16),
            pltpu.VMEM(pair, BF16),
            pltpu.VMEM(pair, BF16),
            pltpu.VMEM((count, HD, slots), F32),
            pltpu.VMEM((count, HD, slots), F32),
            pltpu.VMEM((count, HD, BLOCK), F32),
            pltpu.VMEM((count, HD, BLOCK), F32),
            pltpu.VMEM((BLOCK, width), F32),
            dma((count,)), dma((count,)), dma((count,)), dma((count,)), dma((count,)), dma((count,)),
            dma((HOPS,)), dma((HOPS,)),
        ],
        compiler_params=pltpu.CompilerParams(
            collective_id=0, has_side_effects=True, vmem_limit_bytes=56 * 1024 * 1024
        ),
        cost_estimate=pl.CostEstimate(flops=4 * 10**9, bytes_accessed=20 * 10**6, transcendentals=0),
    )(plan, keep, up, wo, wi, *fwd)


def per_device(key_blocks, ranker, section_inputs, output_grad, input_proj, output_proj, norm_gain):
    count = lax.axis_size("ctx")
    c = lax.axis_index("ctx")
    x = section_inputs[0, 0]
    width = x.shape[1]
    blocks = key_blocks[0]
    wi = input_proj[0].reshape(count, 4, HD, width)
    gain = lax.dynamic_slice_in_dim(norm_gain[0], c * HD, HD)
    x_all = lax.all_gather(x, "ctx", axis=0, tiled=False)
    proj = jnp.einsum("rd,ned->nre", input_proj[0], x[None], preferred_element_type=F32).astype(BF16)
    proj = proj.reshape(count, 4 * HD, BLOCK)
    proj = lax.all_to_all(proj, "ctx", split_axis=0, concat_axis=0, tiled=True)
    fwd = forward(proj, gain, blocks, ranker[0])
    plan, keep = segment_plan(blocks[:, 2])
    sg, gpa, gpb = run_chain(plan, keep, output_grad[0], output_proj[0], wi, fwd)
    factor = float(count * BLOCK) ** (-0.5)
    wa = jnp.einsum("nre,ned->rd", gpa, x_all, preferred_element_type=F32) * factor
    wb = jnp.einsum("nre,ned->rd", gpb, x_all, preferred_element_type=F32) * factor
    weight = jnp.concatenate([wa[:HD], wb[:HD], wa[HD:], wb[HD:]], axis=0)
    return sg[None, None], weight[None]


def solution(mesh):
    placed = (
        P(),
        P(),
        P("pipe", None, "ctx", None),
        P(None, "ctx", None),
        P("pipe", None, None),
        P("pipe", None, None),
        P("pipe", None),
    )
    return jax.shard_map(
        per_device,
        mesh=mesh,
        in_specs=placed,
        out_specs=(P("pipe", None, "ctx", None), P("pipe", "ctx", None)),
        check_vma=False,
    )
```

```python
import math

import jax
import jax.numpy as jnp
from jax import lax
from jax.experimental import pallas as pl
from jax.experimental.pallas import tpu as pltpu
from jax.sharding import PartitionSpec as P

BLOCK = 128
HD = 64
CHUNKS = 4
LATE = 3
MESH = pl.DeviceIdType.MESH
F32 = jnp.float32
BF16 = jnp.bfloat16


def segment_plan(third):
    count = third.shape[0]
    ids = jnp.arange(count, dtype=jnp.int32)
    before = (third[None, :] < third[:, None]) | ((third[None, :] == third[:, None]) & (ids[None, :] < ids[:, None]))
    place = jnp.sum(before.astype(jnp.int32), axis=1)
    order = jnp.sum(jnp.where(place[None, :] == ids[:, None], ids[None, :], 0), axis=1)
    ordered = jnp.sum(jnp.where(place[None, :] == ids[:, None], third[None, :], 0), axis=1)
    keep = (ordered == jnp.concatenate([ordered[:1] - 1, ordered[:-1]])).astype(F32)
    upto = jnp.sum((third[None, :] <= ids[:, None]).astype(jnp.int32), axis=1)
    has = jnp.any(third[None, :] == ids[:, None], axis=1).astype(F32)
    last = jnp.maximum(upto - 1, 0)
    return jnp.stack([order, last]), jnp.stack([keep, has])


def dot(left, right):
    return jnp.dot(left, right, preferred_element_type=F32)


def ntdot(left, right):
    return lax.dot_general(left, right, (((1,), (1,)), ((), ())), preferred_element_type=F32)


def tdot(left, right):
    return lax.dot_general(left, right, (((0,), (0,)), ((), ())), preferred_element_type=F32)


def kernel(
    blocks_ref, order_ref, keep_ref, up_ref, gain_ref, row_ref, col_ref, x_ref, wi_ref, wo_ref,
    sg_ref, dw_ref,
    xv, xt, wi, wo_own, wo_next, psend, pin, xall, gate, query, key, value, keyt, valuet, weight, slope,
    ahead, normed, fac, upbuf, sgsend, cotfirst, cotsend, cotin, gpa, gpb, gain_a, gain_b, gvt, gkt, segv, segk, acc,
    xl, wil, wol, ps, pr, fs, cs, cr, as_, ar, bs, br, xs, xr, us, ur, ws, wr,
):
    count, _, width = xall.shape
    side = math.isqrt(count)
    per_chunk = count // CHUNKS
    s = lax.axis_index("pipe")
    c = lax.axis_index("ctx")
    sections = lax.axis_size("pipe")
    first = s == sections - 1
    cy, cz = c // side, lax.rem(c, side)

    def to(d):
        return lax.rem(cy + d // side, side) * side + lax.rem(cz + d % side, side)

    def source(d):
        return lax.rem(cy + side - d // side, side) * side + lax.rem(cz + side - d % side, side)

    def distance(d):
        y, z = d // side, d % side
        return min(y, side - y) + min(z, side - z)

    near = sorted(range(count), key=distance)
    far = [d for d in near[::-1] if d]

    def remote(src, dst, send, recv, where):
        return pltpu.make_async_remote_copy(
            src_ref=src, dst_ref=dst, send_sem=send, recv_sem=recv, device_id=where, device_id_type=MESH
        )

    x_load = pltpu.make_async_copy(x_ref, xv, xl)
    wo_load = pltpu.make_async_copy(wo_ref, wo_own, wol)

    def wi_load(k):
        span = pl.ds(k * per_chunk, per_chunk)
        return pltpu.make_async_copy(wi_ref.at[span], wi.at[span], wil.at[k])

    def chunk_at(i):
        return lax.rem(c // per_chunk + i, CHUNKS)

    x_load.start()

    @pl.when(first)
    def _():
        wo_load.start()

    for i in range(CHUNKS):
        wi_load(chunk_at(i)).start()

    barrier = pltpu.get_barrier_semaphore()
    after, before = lax.rem(s + 1, sections), lax.rem(s + sections - 1, sections)
    pl.semaphore_signal(barrier, inc=1, device_id=(before, c), device_id_type=MESH)
    for d in range(1, count):
        pl.semaphore_signal(barrier, inc=1, device_id=(s, to(d)), device_id_type=MESH)
    for h in range(count):
        pl.semaphore_signal(barrier, inc=1, device_id=(after, h), device_id_type=MESH)
    pl.semaphore_wait(barrier, 2 * count)

    wo_push = remote(wo_ref, wo_next, ws, wr, (after, c))

    @pl.when(jnp.logical_not(first))
    def _():
        wo_push.start()

    def first_copy(d):
        h = to(d)
        return remote(cotfirst.at[h], cotin.at[c], fs.at[d], cr.at[d], (s, h))

    def cot_copy(d):
        h = to(d)
        return remote(cotsend.at[h], cotin.at[c], cs.at[d], cr.at[d], (before, h))

    def cot_arrival(d):
        n = source(d)
        return remote(cotsend.at[n], cotin.at[n], cs.at[d], cr.at[d], (s, n))

    def set_cot(held, cot):
        held[...] = cot.T.astype(BF16).reshape(count, HD, BLOCK)

    @pl.when(first)
    def _():
        wo_load.wait()
        set_cot(cotfirst, dot(up_ref[...], wo_own[...]))
        for d in far:
            first_copy(d).start()
        cotin[c] = cotfirst[c]
        upbuf[...] = up_ref[...]

    def p_copy(h):
        return remote(psend.at[h], pin.at[c], ps.at[h], pr.at[c], (s, h))

    def p_arrival(h):
        return remote(psend.at[h], pin.at[h], ps.at[h], pr.at[h], (s, h))

    x_load.wait()
    xt[...] = xv[...].T

    def project(i, carry):
        k = chunk_at(i)
        span = pl.ds(k * per_chunk, per_chunk)
        wi_load(k).wait()
        rows = wi[span].reshape(per_chunk * 4 * HD, width)
        psend[span] = dot(rows, xt[...]).astype(BF16).reshape(per_chunk, 4 * HD, BLOCK)
        for j in range(per_chunk):
            h = k * per_chunk + j

            @pl.when(h != c)
            def _(h=h):
                p_copy(h).start()

        return carry

    lax.fori_loop(0, CHUNKS, project, 0)
    pin[c] = psend[c]

    def x_copy(d):
        h = to(d)
        return remote(xv, xall.at[c], xs.at[d], xr.at[d], (s, h))

    def x_arrival(d):
        n = source(d)
        return remote(xv, xall.at[n], xs.at[d], xr.at[d], (s, n))

    def activate(d):
        n = source(d)
        if d:
            p_arrival(n).wait_recv()
        pre = pin[n].astype(F32)
        sigma = jax.nn.sigmoid(pre)
        act = (pre * sigma).astype(BF16)
        slopes = sigma * (1.0 + pre * (1.0 - sigma))
        gate[n] = act[:HD]
        value[n] = act[HD : 2 * HD]
        query[n] = act[2 * HD : 3 * HD]
        key[n] = act[3 * HD :]
        valuet[n] = act[HD : 2 * HD].astype(F32).T.astype(BF16)
        keyt[n] = act[3 * HD :].astype(F32).T.astype(BF16)
        fac[n, 0] = slopes[:HD]
        fac[n, 1] = slopes[2 * HD : 3 * HD]
        fac[n, 2] = slopes[HD : 2 * HD]
        fac[n, 3] = slopes[3 * HD :]

    for d in near:
        activate(d)

    @pl.when(s < LATE)
    def _():
        for d in far:
            x_copy(d).start()

    xall[c] = xv[...]
    scale = HD ** (-0.5)
    gain = gain_ref[...]
    apart = lax.broadcasted_iota(jnp.int32, (BLOCK, BLOCK), 0) - lax.broadcasted_iota(jnp.int32, (BLOCK, BLOCK), 1)

    def slots(n):
        return [blocks_ref[n, t] for t in range(3)]

    def attend(n, carry):
        listed = slots(n)
        at = [jnp.maximum(b, 0) for b in listed]
        scores = dot(jnp.concatenate([keyt[m] for m in at], axis=0), query[n]) * scale
        rank = row_ref[n]
        allowed = jnp.concatenate(
            [
                (apart <= (n - b) * BLOCK) & (col_ref[m] == jnp.where(b >= 0, rank, -1.0))
                for b, m in zip(listed, at)
            ],
            axis=0,
        )
        sigma = jax.nn.sigmoid(scores)
        now = jnp.where(allowed, scores * sigma, 0.0).astype(BF16)
        weight[n] = now
        slope[n] = (jnp.where(allowed, sigma * (1.0 + scores * (1.0 - sigma)), 0.0) * scale).astype(BF16)
        attended = dot(jnp.concatenate([value[m] for m in at], axis=1), now)
        inv_rms = lax.rsqrt(jnp.sum(attended * attended, axis=0, keepdims=True) * (1.0 / HD) + 1.0)
        norm = attended * inv_rms
        normed[n] = norm
        ahead[n] = inv_rms * gain * gate[n].astype(F32)
        fac[n, 0] = gain * norm * fac[n, 0]
        return carry

    lax.fori_loop(0, count, attend, 0, unroll=2)

    def back_copy(src, landing, send, recv, d):
        n = source(d)
        return remote(src.at[n], landing.at[c], send.at[d], recv.at[d], (s, n))

    def back_arrival(src, landing, send, recv, d):
        h = to(d)
        return remote(src.at[h], landing.at[h], send.at[d], recv.at[d], (s, h))

    def head(d):
        n = source(d)
        at = [jnp.maximum(b, 0) for b in slots(n)]
        cot_n = cotin[n].astype(F32)
        norm = normed[n]
        steep = cot_n * ahead[n]
        mean = jnp.sum(steep * norm, axis=0, keepdims=True) * (1.0 / HD)
        ga = (steep - norm * mean).astype(BF16)
        gw = dot(jnp.concatenate([valuet[m] for m in at], axis=0), ga)
        gs = (gw * slope[n].astype(F32)).astype(BF16)
        gq = dot(jnp.concatenate([key[m] for m in at], axis=1), gs)
        gpa[n, :HD] = (cot_n * fac[n, 0]).astype(BF16)
        gpa[n, HD:] = (gq * fac[n, 1]).astype(BF16)
        gvt[n] = ntdot(ga, weight[n])
        gkt[n] = ntdot(query[n], gs)

    group = 4
    for g in range(0, count, group):
        for d in near[g : g + group]:
            if d:
                cot_arrival(d).wait_recv()
            else:

                @pl.when(jnp.logical_not(first))
                def _(d=d):
                    cot_arrival(d).wait_recv()

        for d in near[g : g + group]:
            head(d)
        for d in near[g : g + group]:
            if d:
                back_copy(gpa, gain_a, as_, ar, d).start()
    gain_a[c] = gpa[c]

    def seg_step(i, carry):
        run_v, run_k = carry
        n = order_ref[0, i]
        keep = keep_ref[0, i]
        run_v = run_v * keep + gvt[n, :, 2 * BLOCK :]
        run_k = run_k * keep + gkt[n, :, 2 * BLOCK :]
        segv[i] = run_v
        segk[i] = run_k
        return run_v, run_k

    zero = jnp.zeros((HD, BLOCK), F32)
    lax.fori_loop(0, count, seg_step, (zero, zero), unroll=2)

    def finalise(d):
        m = source(d)
        later = lax.rem(m + 1, count)
        last = order_ref[1, m]
        has = keep_ref[1, m]
        gv = gvt[m, :, :BLOCK] + gvt[later, :, BLOCK : 2 * BLOCK] + segv[last] * has
        gk = gkt[m, :, :BLOCK] + gkt[later, :, BLOCK : 2 * BLOCK] + segk[last] * has
        gpb[m, :HD] = (gv * fac[m, 2]).astype(BF16)
        gpb[m, HD:] = (gk * fac[m, 3]).astype(BF16)

    for d in far:
        finalise(d)
        back_copy(gpb, gain_b, bs, br, d).start()
    finalise(0)
    gain_b[c] = gpb[c]

    norm_factor = float(count * BLOCK) ** (-0.5)

    def weight_grad():
        for d in far[::-1]:
            x_arrival(d).wait_recv()
        whole = xall[...].reshape(count * BLOCK, width)
        for src, base in ((gpa, 0), (gpb, HD)):
            part = dot(jnp.concatenate([src[n] for n in range(count)], axis=1), whole) * norm_factor
            dw_ref[base : base + HD] = part[:HD]
            dw_ref[base + 2 * HD : base + 3 * HD] = part[HD:]

    def half_weights(parts, span):
        return jnp.concatenate([wi[h, p, :, span] for h in range(count) for p in parts], axis=0)

    for d in near[1:]:
        back_arrival(gpa, gain_a, as_, ar, d).wait_recv()
    left = gain_a[...].reshape(count * BLOCK, BLOCK)

    @pl.when(jnp.logical_not(first))
    def _():
        remote(sgsend, upbuf, us, ur, (s, c)).wait_recv()
        wo_push.wait_send()
    acc[...] = upbuf[...].astype(F32) + tdot(left, half_weights((0, 2), slice(None)))

    @pl.when(s < LATE)
    def _():
        weight_grad()

    @pl.when(s > 0)
    def _():
        remote(wo_ref, wo_next, ws, wr, (s, c)).wait_recv()

    for d in near[1:]:
        back_arrival(gpb, gain_b, bs, br, d).wait_recv()
    left = gain_b[...].reshape(count * BLOCK, BLOCK)
    cols = width // CHUNKS
    for i in range(CHUNKS):
        span = slice(i * cols, (i + 1) * cols)
        part = (acc[:, span] + tdot(left, half_weights((1, 3), span))).astype(BF16)
        sgsend[:, span] = part
        sg_ref[:, span] = part

    up_push = remote(sgsend, upbuf, us, ur, (before, c))

    @pl.when(s > 0)
    def _():
        set_cot(cotsend, dot(sgsend[...], wo_next[...]))
        for d in far + [0]:
            cot_copy(d).start()
        up_push.start()

    @pl.when(s >= LATE)
    def _():
        for d in far:
            x_copy(d).start()
        weight_grad()

    @pl.when(first)
    def _():
        for d in far:
            first_copy(d).wait_send()

    for d in far:
        p_copy(to(d)).wait_send()
        back_copy(gpa, gain_a, as_, ar, d).wait_send()
        back_copy(gpb, gain_b, bs, br, d).wait_send()
        x_copy(d).wait_send()

    @pl.when(s > 0)
    def _():
        for d in far + [0]:
            cot_copy(d).wait_send()
        up_push.wait_send()


def per_device(key_blocks, ranker, section_inputs, output_grad, input_proj, output_proj, norm_gain):
    count = lax.axis_size("ctx")
    c = lax.axis_index("ctx")
    x = section_inputs[0, 0]
    width = x.shape[1]
    blocks = key_blocks[0]
    gain = lax.dynamic_slice_in_dim(norm_gain[0], c * HD, HD)
    gain = jnp.broadcast_to(gain[:, None], (HD, BLOCK))
    ranks = ranker[0].reshape(count, BLOCK).astype(F32)
    order, keep = segment_plan(blocks[:, 2])
    vmem = pl.BlockSpec(memory_space=pltpu.VMEM)
    smem = pl.BlockSpec(memory_space=pltpu.SMEM)
    hbm = pl.BlockSpec(memory_space=pl.ANY)
    dma = pltpu.SemaphoreType.DMA
    full = 3 * BLOCK

    def half(*shape):
        return pltpu.VMEM(shape, BF16)

    def single(*shape):
        return pltpu.VMEM(shape, F32)

    sg, dw = pl.pallas_call(
        kernel,
        out_shape=(
            jax.ShapeDtypeStruct((BLOCK, width), BF16),
            jax.ShapeDtypeStruct((4 * HD, width), F32),
        ),
        in_specs=[smem, smem, smem, vmem, vmem, vmem, vmem, hbm, hbm, hbm],
        out_specs=(vmem, vmem),
        scratch_shapes=[
            half(BLOCK, width),
            half(width, BLOCK),
            half(count, 4, HD, width),
            half(width, width),
            half(width, width),
            half(count, 4 * HD, BLOCK),
            half(count, 4 * HD, BLOCK),
            half(count, BLOCK, width),
            half(count, HD, BLOCK),
            half(count, HD, BLOCK),
            half(count, HD, BLOCK),
            half(count, HD, BLOCK),
            half(count, BLOCK, HD),
            half(count, BLOCK, HD),
            half(count, full, BLOCK),
            half(count, full, BLOCK),
            single(count, HD, BLOCK),
            single(count, HD, BLOCK),
            single(count, 4, HD, BLOCK),
            half(BLOCK, width),
            half(BLOCK, width),
            half(count, HD, BLOCK),
            half(count, HD, BLOCK),
            half(count, HD, BLOCK),
            half(count, 2 * HD, BLOCK),
            half(count, 2 * HD, BLOCK),
            half(count, 2 * HD, BLOCK),
            half(count, 2 * HD, BLOCK),
            single(count, HD, full),
            single(count, HD, full),
            single(count, HD, BLOCK),
            single(count, HD, BLOCK),
            single(BLOCK, width),
            dma,
            dma((CHUNKS,)),
            dma,
        ]
        + [dma((count,)) for _ in range(11)]
        + [dma for _ in range(4)],
        compiler_params=pltpu.CompilerParams(
            collective_id=0, has_side_effects=True, vmem_limit_bytes=58 * 1024 * 1024
        ),
        cost_estimate=pl.CostEstimate(flops=5 * 10**9, bytes_accessed=20 * 10**6, transcendentals=0),
    )(
        blocks, order, keep, output_grad[0], gain, ranks[:, None, :], ranks[:, :, None],
        x, input_proj[0].reshape(count, 4, HD, width), output_proj[0],
    )
    return sg[None, None], dw[None]


def solution(mesh):
    placed = (
        P(),
        P(),
        P("pipe", None, "ctx", None),
        P(None, "ctx", None),
        P("pipe", None, None),
        P("pipe", None, None),
        P("pipe", None),
    )
    return jax.shard_map(
        per_device,
        mesh=mesh,
        in_specs=placed,
        out_specs=(P("pipe", None, "ctx", None), P("pipe", "ctx", None)),
        check_vma=False,
    )
```

```python
import math

import jax
import jax.numpy as jnp
from jax import lax
from jax.experimental import pallas as pl
from jax.experimental.pallas import tpu as pltpu
from jax.sharding import PartitionSpec as P

BLOCK = 128
HD = 64
CHUNKS = 4
MESH = pl.DeviceIdType.MESH
F32 = jnp.float32
BF16 = jnp.bfloat16


def segment_plan(third):
    count = third.shape[0]
    ids = jnp.arange(count, dtype=jnp.int32)
    before = (third[None, :] < third[:, None]) | ((third[None, :] == third[:, None]) & (ids[None, :] < ids[:, None]))
    place = jnp.sum(before.astype(jnp.int32), axis=1)
    order = jnp.sum(jnp.where(place[None, :] == ids[:, None], ids[None, :], 0), axis=1)
    ordered = jnp.sum(jnp.where(place[None, :] == ids[:, None], third[None, :], 0), axis=1)
    keep = (ordered == jnp.concatenate([ordered[:1] - 1, ordered[:-1]])).astype(F32)
    upto = jnp.sum((third[None, :] <= ids[:, None]).astype(jnp.int32), axis=1)
    has = jnp.any(third[None, :] == ids[:, None], axis=1).astype(F32)
    last = jnp.maximum(upto - 1, 0)
    return jnp.stack([order, last]), jnp.stack([keep, has])


def dot(left, right):
    return jnp.dot(left, right, preferred_element_type=F32)


def ntdot(left, right):
    return lax.dot_general(left, right, (((1,), (1,)), ((), ())), preferred_element_type=F32)


def tdot(left, right):
    return lax.dot_general(left, right, (((0,), (0,)), ((), ())), preferred_element_type=F32)


def kernel(
    blocks_ref, order_ref, keep_ref, up_ref, gain_ref, row_ref, col_ref, x_ref, wi_ref, wo_ref,
    sg_ref, dw_ref,
    xv, xt, wi, wo_own, wo_next, psend, pin, xall, gate, query, key, value, keyt, valuet, weight, slope,
    ahead, normed, fac, upbuf, sgsend, cotfirst, cotsend, cotin, gpa, gpb, gain_a, gain_b, gvt, gkt, segv, segk, acc,
    xl, wil, wol, ps, pr, fs, cs, cr, as_, ar, bs, br, xs, xr, us, ur, ws, wr, go,
):
    count, _, width = xall.shape
    side = math.isqrt(count)
    per_chunk = count // CHUNKS
    s = lax.axis_index("pipe")
    c = lax.axis_index("ctx")
    sections = lax.axis_size("pipe")
    first = s == sections - 1
    second = s == sections - 2
    late = first | second | (s == sections - 4)
    cy, cz = c // side, lax.rem(c, side)

    def to(d):
        return lax.rem(cy + d // side, side) * side + lax.rem(cz + d % side, side)

    def source(d):
        return lax.rem(cy + side - d // side, side) * side + lax.rem(cz + side - d % side, side)

    def distance(d):
        y, z = d // side, d % side
        return min(y, side - y) + min(z, side - z)

    near = sorted(range(count), key=distance)
    far = [d for d in near[::-1] if d]

    def remote(src, dst, send, recv, where):
        return pltpu.make_async_remote_copy(
            src_ref=src, dst_ref=dst, send_sem=send, recv_sem=recv, device_id=where, device_id_type=MESH
        )

    x_load = pltpu.make_async_copy(x_ref, xv, xl)
    wo_load = pltpu.make_async_copy(wo_ref, wo_own, wol)

    def wi_load(k):
        span = pl.ds(k * per_chunk, per_chunk)
        return pltpu.make_async_copy(wi_ref.at[span], wi.at[span], wil.at[k])

    def chunk_at(i):
        return lax.rem(c // per_chunk + i, CHUNKS)

    x_load.start()

    @pl.when(first)
    def _():
        wo_load.start()

    for i in range(CHUNKS):
        wi_load(chunk_at(i)).start()

    barrier = pltpu.get_barrier_semaphore()
    after, before = lax.rem(s + 1, sections), lax.rem(s + sections - 1, sections)
    pl.semaphore_signal(barrier, inc=1, device_id=(before, c), device_id_type=MESH)
    for d in range(1, count):
        pl.semaphore_signal(barrier, inc=1, device_id=(s, to(d)), device_id_type=MESH)
    for h in range(count):
        pl.semaphore_signal(barrier, inc=1, device_id=(after, h), device_id_type=MESH)
    pl.semaphore_wait(barrier, 2 * count)

    wo_push = remote(wo_ref, wo_next, ws, wr, (after, c))

    @pl.when(jnp.logical_not(first))
    def _():
        wo_push.start()

    def first_copy(d):
        h = to(d)
        return remote(cotfirst.at[h], cotin.at[c], fs.at[d], cr.at[d], (s, h))

    def cot_copy(d):
        h = to(d)
        return remote(cotsend.at[h], cotin.at[c], cs.at[d], cr.at[d], (before, h))

    def cot_arrival(d):
        n = source(d)
        return remote(cotsend.at[n], cotin.at[n], cs.at[d], cr.at[d], (s, n))

    def set_cot(held, cot):
        held[...] = cot.T.astype(BF16).reshape(count, HD, BLOCK)

    def p_copy(h):
        return remote(psend.at[h], pin.at[c], ps.at[h], pr.at[c], (s, h))

    def p_arrival(h):
        return remote(psend.at[h], pin.at[h], ps.at[h], pr.at[h], (s, h))

    x_load.wait()
    xt[...] = xv[...].T

    def project(i, carry):
        k = chunk_at(i)
        span = pl.ds(k * per_chunk, per_chunk)
        wi_load(k).wait()
        rows = wi[span].reshape(per_chunk * 4 * HD, width)
        psend[span] = dot(rows, xt[...]).astype(BF16).reshape(per_chunk, 4 * HD, BLOCK)
        for j in range(per_chunk):
            h = k * per_chunk + j

            @pl.when(h != c)
            def _(h=h):
                p_copy(h).start()

        return carry

    @pl.when(second)
    def _():
        pl.semaphore_wait(go, 1)

    lax.fori_loop(0, CHUNKS, project, 0)
    pin[c] = psend[c]

    @pl.when(first)
    def _():
        wo_load.wait()
        set_cot(cotfirst, dot(up_ref[...], wo_own[...]))
        for d in far:
            first_copy(d).start()
        cotin[c] = cotfirst[c]
        upbuf[...] = up_ref[...]

    def x_copy(d):
        h = to(d)
        return remote(xv, xall.at[c], xs.at[d], xr.at[d], (s, h))

    def x_arrival(d):
        n = source(d)
        return remote(xv, xall.at[n], xs.at[d], xr.at[d], (s, n))

    def activate(d):
        n = source(d)
        if d:
            p_arrival(n).wait_recv()
        pre = pin[n].astype(F32)
        sigma = jax.nn.sigmoid(pre)
        act = (pre * sigma).astype(BF16)
        slopes = sigma * (1.0 + pre * (1.0 - sigma))
        gate[n] = act[:HD]
        value[n] = act[HD : 2 * HD]
        query[n] = act[2 * HD : 3 * HD]
        key[n] = act[3 * HD :]
        valuet[n] = act[HD : 2 * HD].astype(F32).T.astype(BF16)
        keyt[n] = act[3 * HD :].astype(F32).T.astype(BF16)
        fac[n, 0] = slopes[:HD]
        fac[n, 1] = slopes[2 * HD : 3 * HD]
        fac[n, 2] = slopes[HD : 2 * HD]
        fac[n, 3] = slopes[3 * HD :]

    for d in near:
        activate(d)

    @pl.when(first)
    def _():
        pl.semaphore_signal(go, inc=1, device_id=(before, c), device_id_type=MESH)

    @pl.when(jnp.logical_not(late))
    def _():
        for d in far:
            x_copy(d).start()

    xall[c] = xv[...]
    scale = HD ** (-0.5)
    gain = gain_ref[...]
    apart = lax.broadcasted_iota(jnp.int32, (BLOCK, BLOCK), 0) - lax.broadcasted_iota(jnp.int32, (BLOCK, BLOCK), 1)

    def slots(n):
        return [blocks_ref[n, t] for t in range(3)]

    def attend(n, carry):
        listed = slots(n)
        at = [jnp.maximum(b, 0) for b in listed]
        scores = dot(jnp.concatenate([keyt[m] for m in at], axis=0), query[n]) * scale
        rank = row_ref[n]
        allowed = jnp.concatenate(
            [
                (apart <= (n - b) * BLOCK) & (col_ref[m] == jnp.where(b >= 0, rank, -1.0))
                for b, m in zip(listed, at)
            ],
            axis=0,
        )
        sigma = jax.nn.sigmoid(scores)
        now = jnp.where(allowed, scores * sigma, 0.0).astype(BF16)
        weight[n] = now
        slope[n] = (jnp.where(allowed, sigma * (1.0 + scores * (1.0 - sigma)), 0.0) * scale).astype(BF16)
        attended = dot(jnp.concatenate([value[m] for m in at], axis=1), now)
        inv_rms = lax.rsqrt(jnp.sum(attended * attended, axis=0, keepdims=True) * (1.0 / HD) + 1.0)
        norm = attended * inv_rms
        normed[n] = norm
        ahead[n] = inv_rms * gain * gate[n].astype(F32)
        fac[n, 0] = gain * norm * fac[n, 0]
        return carry

    lax.fori_loop(0, count, attend, 0, unroll=2)

    def back_copy(src, landing, send, recv, d):
        n = source(d)
        return remote(src.at[n], landing.at[c], send.at[d], recv.at[d], (s, n))

    def back_arrival(src, landing, send, recv, d):
        h = to(d)
        return remote(src.at[h], landing.at[h], send.at[d], recv.at[d], (s, h))

    def head(d):
        n = source(d)
        at = [jnp.maximum(b, 0) for b in slots(n)]
        cot_n = cotin[n].astype(F32)
        norm = normed[n]
        steep = cot_n * ahead[n]
        mean = jnp.sum(steep * norm, axis=0, keepdims=True) * (1.0 / HD)
        ga = (steep - norm * mean).astype(BF16)
        gw = dot(jnp.concatenate([valuet[m] for m in at], axis=0), ga)
        gs = (gw * slope[n].astype(F32)).astype(BF16)
        gq = dot(jnp.concatenate([key[m] for m in at], axis=1), gs)
        gpa[n, :HD] = (cot_n * fac[n, 0]).astype(BF16)
        gpa[n, HD:] = (gq * fac[n, 1]).astype(BF16)
        gvt[n] = ntdot(ga, weight[n])
        gkt[n] = ntdot(query[n], gs)

    group = 4
    for g in range(0, count, group):
        for d in near[g : g + group]:
            if d:
                cot_arrival(d).wait_recv()
            else:

                @pl.when(jnp.logical_not(first))
                def _(d=d):
                    cot_arrival(d).wait_recv()

        for d in near[g : g + group]:
            head(d)
        for d in near[g : g + group]:
            if d:
                back_copy(gpa, gain_a, as_, ar, d).start()
    gain_a[c] = gpa[c]

    def seg_step(i, carry):
        run_v, run_k = carry
        n = order_ref[0, i]
        keep = keep_ref[0, i]
        run_v = run_v * keep + gvt[n, :, 2 * BLOCK :]
        run_k = run_k * keep + gkt[n, :, 2 * BLOCK :]
        segv[i] = run_v
        segk[i] = run_k
        return run_v, run_k

    zero = jnp.zeros((HD, BLOCK), F32)
    lax.fori_loop(0, count, seg_step, (zero, zero), unroll=2)

    def finalise(d):
        m = source(d)
        later = lax.rem(m + 1, count)
        last = order_ref[1, m]
        has = keep_ref[1, m]
        gv = gvt[m, :, :BLOCK] + gvt[later, :, BLOCK : 2 * BLOCK] + segv[last] * has
        gk = gkt[m, :, :BLOCK] + gkt[later, :, BLOCK : 2 * BLOCK] + segk[last] * has
        gpb[m, :HD] = (gv * fac[m, 2]).astype(BF16)
        gpb[m, HD:] = (gk * fac[m, 3]).astype(BF16)

    for d in far:
        finalise(d)
        back_copy(gpb, gain_b, bs, br, d).start()
    finalise(0)
    gain_b[c] = gpb[c]

    norm_factor = float(count * BLOCK) ** (-0.5)

    def weight_grad():
        for d in far[::-1]:
            x_arrival(d).wait_recv()
        whole = xall[...].reshape(count * BLOCK, width)
        for src, base in ((gpa, 0), (gpb, HD)):
            part = dot(jnp.concatenate([src[n] for n in range(count)], axis=1), whole) * norm_factor
            dw_ref[base : base + HD] = part[:HD]
            dw_ref[base + 2 * HD : base + 3 * HD] = part[HD:]

    def half_weights(parts, span):
        return jnp.concatenate([wi[h, p, :, span] for h in range(count) for p in parts], axis=0)

    for d in near[1:]:
        back_arrival(gpa, gain_a, as_, ar, d).wait_recv()
    left = gain_a[...].reshape(count * BLOCK, BLOCK)

    @pl.when(jnp.logical_not(first))
    def _():
        remote(sgsend, upbuf, us, ur, (s, c)).wait_recv()
        wo_push.wait_send()
    acc[...] = upbuf[...].astype(F32) + tdot(left, half_weights((0, 2), slice(None)))

    @pl.when(jnp.logical_not(late))
    def _():
        weight_grad()

    @pl.when(s > 0)
    def _():
        remote(wo_ref, wo_next, ws, wr, (s, c)).wait_recv()

    for d in near[1:]:
        back_arrival(gpb, gain_b, bs, br, d).wait_recv()
    left = gain_b[...].reshape(count * BLOCK, BLOCK)
    cols = width // CHUNKS
    for i in range(CHUNKS):
        span = slice(i * cols, (i + 1) * cols)
        part = (acc[:, span] + tdot(left, half_weights((1, 3), span))).astype(BF16)
        sgsend[:, span] = part
        sg_ref[:, span] = part

    up_push = remote(sgsend, upbuf, us, ur, (before, c))

    @pl.when(s > 0)
    def _():
        set_cot(cotsend, dot(sgsend[...], wo_next[...]))
        for d in far + [0]:
            cot_copy(d).start()
        up_push.start()

    @pl.when(second)
    def _():
        pl.semaphore_signal(go, inc=1, device_id=(after, c), device_id_type=MESH)

    @pl.when(first)
    def _():
        pl.semaphore_wait(go, 1)

    @pl.when(late)
    def _():
        for d in far:
            x_copy(d).start()
        weight_grad()

    @pl.when(first)
    def _():
        for d in far:
            first_copy(d).wait_send()

    for d in far:
        p_copy(to(d)).wait_send()
        back_copy(gpa, gain_a, as_, ar, d).wait_send()
        back_copy(gpb, gain_b, bs, br, d).wait_send()
        x_copy(d).wait_send()

    @pl.when(s > 0)
    def _():
        for d in far + [0]:
            cot_copy(d).wait_send()
        up_push.wait_send()


def per_device(key_blocks, ranker, section_inputs, output_grad, input_proj, output_proj, norm_gain):
    count = lax.axis_size("ctx")
    c = lax.axis_index("ctx")
    x = section_inputs[0, 0]
    width = x.shape[1]
    blocks = key_blocks[0]
    gain = lax.dynamic_slice_in_dim(norm_gain[0], c * HD, HD)
    gain = jnp.broadcast_to(gain[:, None], (HD, BLOCK))
    ranks = ranker[0].reshape(count, BLOCK).astype(F32)
    order, keep = segment_plan(blocks[:, 2])
    vmem = pl.BlockSpec(memory_space=pltpu.VMEM)
    smem = pl.BlockSpec(memory_space=pltpu.SMEM)
    hbm = pl.BlockSpec(memory_space=pl.ANY)
    dma = pltpu.SemaphoreType.DMA
    full = 3 * BLOCK

    def half(*shape):
        return pltpu.VMEM(shape, BF16)

    def single(*shape):
        return pltpu.VMEM(shape, F32)

    sg, dw = pl.pallas_call(
        kernel,
        out_shape=(
            jax.ShapeDtypeStruct((BLOCK, width), BF16),
            jax.ShapeDtypeStruct((4 * HD, width), F32),
        ),
        in_specs=[smem, smem, smem, vmem, vmem, vmem, vmem, hbm, hbm, hbm],
        out_specs=(vmem, vmem),
        scratch_shapes=[
            half(BLOCK, width),
            half(width, BLOCK),
            half(count, 4, HD, width),
            half(width, width),
            half(width, width),
            half(count, 4 * HD, BLOCK),
            half(count, 4 * HD, BLOCK),
            half(count, BLOCK, width),
            half(count, HD, BLOCK),
            half(count, HD, BLOCK),
            half(count, HD, BLOCK),
            half(count, HD, BLOCK),
            half(count, BLOCK, HD),
            half(count, BLOCK, HD),
            half(count, full, BLOCK),
            half(count, full, BLOCK),
            single(count, HD, BLOCK),
            single(count, HD, BLOCK),
            single(count, 4, HD, BLOCK),
            half(BLOCK, width),
            half(BLOCK, width),
            half(count, HD, BLOCK),
            half(count, HD, BLOCK),
            half(count, HD, BLOCK),
            half(count, 2 * HD, BLOCK),
            half(count, 2 * HD, BLOCK),
            half(count, 2 * HD, BLOCK),
            half(count, 2 * HD, BLOCK),
            single(count, HD, full),
            single(count, HD, full),
            single(count, HD, BLOCK),
            single(count, HD, BLOCK),
            single(BLOCK, width),
            dma,
            dma((CHUNKS,)),
            dma,
        ]
        + [dma((count,)) for _ in range(11)]
        + [dma for _ in range(4)]
        + [pltpu.SemaphoreType.REGULAR],
        compiler_params=pltpu.CompilerParams(
            collective_id=0, has_side_effects=True, vmem_limit_bytes=58 * 1024 * 1024
        ),
        cost_estimate=pl.CostEstimate(flops=5 * 10**9, bytes_accessed=20 * 10**6, transcendentals=0),
    )(
        blocks, order, keep, output_grad[0], gain, ranks[:, None, :], ranks[:, :, None],
        x, input_proj[0].reshape(count, 4, HD, width), output_proj[0],
    )
    return sg[None, None], dw[None]


def solution(mesh):
    placed = (
        P(),
        P(),
        P("pipe", None, "ctx", None),
        P(None, "ctx", None),
        P("pipe", None, None),
        P("pipe", None, None),
        P("pipe", None),
    )
    return jax.shard_map(
        per_device,
        mesh=mesh,
        in_specs=placed,
        out_specs=(P("pipe", None, "ctx", None), P("pipe", "ctx", None)),
        check_vma=False,
    )
```

```python
import math

import jax
import jax.numpy as jnp
from jax import lax
from jax.experimental import pallas as pl
from jax.experimental.pallas import tpu as pltpu
from jax.sharding import PartitionSpec as P

BLOCK = 128
HD = 64
CHUNKS = 4
MESH = pl.DeviceIdType.MESH
F32 = jnp.float32
BF16 = jnp.bfloat16


def segment_plan(blocks):
    third = blocks[:, 2]
    count = third.shape[0]
    ids = jnp.arange(count, dtype=jnp.int32)
    before = (third[None, :] < third[:, None]) | ((third[None, :] == third[:, None]) & (ids[None, :] < ids[:, None]))
    place = jnp.sum(before.astype(jnp.int32), axis=1)
    order = jnp.sum(jnp.where(place[None, :] == ids[:, None], ids[None, :], 0), axis=1)
    ordered = jnp.sum(jnp.where(place[None, :] == ids[:, None], third[None, :], 0), axis=1)
    keep = (ordered == jnp.concatenate([ordered[:1] - 1, ordered[:-1]])).astype(jnp.int32)
    upto = jnp.sum((third[None, :] <= ids[:, None]).astype(jnp.int32), axis=1)
    has = jnp.any(third[None, :] == ids[:, None], axis=1).astype(jnp.int32)
    last = jnp.maximum(upto - 1, 0)
    return jnp.concatenate([blocks.T, jnp.stack([order, last, keep, has])], axis=0)


def dot(left, right):
    return jnp.dot(left, right, preferred_element_type=F32)


def ntdot(left, right):
    return lax.dot_general(left, right, (((1,), (1,)), ((), ())), preferred_element_type=F32)


def tdot(left, right):
    return lax.dot_general(left, right, (((0,), (0,)), ((), ())), preferred_element_type=F32)


def kernel(
    plan_ref, up_ref, gain_ref, row_ref, x_ref, wi_ref, wo_ref,
    sg_ref, dw_ref,
    xv, xt, wi, wo_own, wo_next, psend, pin, xall, gate, query, key, value, keyt, valuet, weight, slope,
    ahead, normed, fac, col, upbuf, sgsend, cotfirst, cotsend, cotin, gpa, gpb, gain_a, gain_b, gvt, gkt, segv, segk, acc,
    xl, wil, wol, ps, pr, fs, cs, cr, as_, ar, bs, br, xs, xr, us, ur, ws, wr, go,
):
    count, _, width = xall.shape
    side = math.isqrt(count)
    per_chunk = count // CHUNKS
    s = lax.axis_index("pipe")
    c = lax.axis_index("ctx")
    sections = lax.axis_size("pipe")
    first = s == sections - 1
    second = s == sections - 2
    late = first | second | (s == sections - 4)
    cy, cz = c // side, lax.rem(c, side)

    def to(d):
        return lax.rem(cy + d // side, side) * side + lax.rem(cz + d % side, side)

    def source(d):
        return lax.rem(cy + side - d // side, side) * side + lax.rem(cz + side - d % side, side)

    def distance(d):
        y, z = d // side, d % side
        return min(y, side - y) + min(z, side - z)

    near = sorted(range(count), key=distance)
    far = [d for d in near[::-1] if d]

    def remote(src, dst, send, recv, where):
        return pltpu.make_async_remote_copy(
            src_ref=src, dst_ref=dst, send_sem=send, recv_sem=recv, device_id=where, device_id_type=MESH
        )

    x_load = pltpu.make_async_copy(x_ref, xv, xl)
    wo_load = pltpu.make_async_copy(wo_ref, wo_own, wol)

    def wi_load(k):
        span = pl.ds(k * per_chunk, per_chunk)
        return pltpu.make_async_copy(wi_ref.at[span], wi.at[span], wil.at[k])

    def chunk_at(i):
        return lax.rem(c // per_chunk + i, CHUNKS)

    x_load.start()

    @pl.when(first)
    def _():
        wo_load.start()

    for i in range(CHUNKS):
        wi_load(chunk_at(i)).start()

    barrier = pltpu.get_barrier_semaphore()
    after, before = lax.rem(s + 1, sections), lax.rem(s + sections - 1, sections)
    pl.semaphore_signal(barrier, inc=1, device_id=(before, c), device_id_type=MESH)
    for d in range(1, count):
        pl.semaphore_signal(barrier, inc=1, device_id=(s, to(d)), device_id_type=MESH)
    for h in range(count):
        pl.semaphore_signal(barrier, inc=1, device_id=(after, h), device_id_type=MESH)
    pl.semaphore_wait(barrier, 2 * count)

    wo_push = remote(wo_ref, wo_next, ws, wr, (after, c))

    @pl.when(jnp.logical_not(first))
    def _():
        wo_push.start()

    def first_copy(d):
        h = to(d)
        return remote(cotfirst.at[h], cotin.at[c], fs.at[d], cr.at[d], (s, h))

    def cot_copy(d):
        h = to(d)
        return remote(cotsend.at[h], cotin.at[c], cs.at[d], cr.at[d], (before, h))

    def cot_arrival(d):
        n = source(d)
        return remote(cotsend.at[n], cotin.at[n], cs.at[d], cr.at[d], (s, n))

    def set_cot(held, cot):
        held[...] = cot.T.astype(BF16).reshape(count, HD, BLOCK)

    def p_copy(h):
        return remote(psend.at[h], pin.at[c], ps.at[h], pr.at[c], (s, h))

    def p_arrival(h):
        return remote(psend.at[h], pin.at[h], ps.at[h], pr.at[h], (s, h))

    x_load.wait()
    xt[...] = xv[...].T

    def project(i, carry):
        k = chunk_at(i)
        span = pl.ds(k * per_chunk, per_chunk)
        wi_load(k).wait()
        rows = wi[span].reshape(per_chunk * 4 * HD, width)
        psend[span] = dot(rows, xt[...]).astype(BF16).reshape(per_chunk, 4 * HD, BLOCK)
        for j in range(per_chunk):
            h = k * per_chunk + j

            @pl.when(h != c)
            def _(h=h):
                p_copy(h).start()

        return carry

    @pl.when(second)
    def _():
        pl.semaphore_wait(go, 1)

    lax.fori_loop(0, CHUNKS, project, 0)
    pin[c] = psend[c]

    @pl.when(first)
    def _():
        wo_load.wait()
        set_cot(cotfirst, dot(up_ref[...], wo_own[...]))
        for d in far:
            first_copy(d).start()
        cotin[c] = cotfirst[c]
        upbuf[...] = up_ref[...]

    def spread(m, carry):
        col[m] = jnp.broadcast_to(row_ref[m].astype(F32), (BLOCK, BLOCK)).T
        return carry

    lax.fori_loop(0, count, spread, 0)

    def x_copy(d):
        h = to(d)
        return remote(xv, xall.at[c], xs.at[d], xr.at[d], (s, h))

    def x_arrival(d):
        n = source(d)
        return remote(xv, xall.at[n], xs.at[d], xr.at[d], (s, n))

    def activate(d):
        n = source(d)
        if d:
            p_arrival(n).wait_recv()
        pre = pin[n].astype(F32)
        sigma = jax.nn.sigmoid(pre)
        act = (pre * sigma).astype(BF16)
        slopes = sigma * (1.0 + pre * (1.0 - sigma))
        gate[n] = act[:HD]
        value[n] = act[HD : 2 * HD]
        query[n] = act[2 * HD : 3 * HD]
        key[n] = act[3 * HD :]
        valuet[n] = act[HD : 2 * HD].astype(F32).T.astype(BF16)
        keyt[n] = act[3 * HD :].astype(F32).T.astype(BF16)
        fac[n, 0] = slopes[:HD]
        fac[n, 1] = slopes[2 * HD : 3 * HD]
        fac[n, 2] = slopes[HD : 2 * HD]
        fac[n, 3] = slopes[3 * HD :]

    for d in near:
        activate(d)

    @pl.when(first)
    def _():
        pl.semaphore_signal(go, inc=1, device_id=(before, c), device_id_type=MESH)

    @pl.when(jnp.logical_not(late))
    def _():
        for d in far:
            x_copy(d).start()

    xall[c] = xv[...]
    scale = HD ** (-0.5)
    gain = jnp.broadcast_to(gain_ref[c], (BLOCK, HD)).T
    apart = lax.broadcasted_iota(jnp.int32, (BLOCK, BLOCK), 0) - lax.broadcasted_iota(jnp.int32, (BLOCK, BLOCK), 1)

    def slots(n):
        return [plan_ref[t, n] for t in range(3)]

    def attend(n, carry):
        listed = slots(n)
        at = [jnp.maximum(b, 0) for b in listed]
        scores = dot(jnp.concatenate([keyt[m] for m in at], axis=0), query[n]) * scale
        rank = row_ref[n].astype(F32)
        allowed = jnp.concatenate(
            [
                (apart <= (n - b) * BLOCK) & (col[m] == jnp.where(b >= 0, rank, -1.0))
                for b, m in zip(listed, at)
            ],
            axis=0,
        )
        sigma = jax.nn.sigmoid(scores)
        now = jnp.where(allowed, scores * sigma, 0.0).astype(BF16)
        weight[n] = now
        slope[n] = (jnp.where(allowed, sigma * (1.0 + scores * (1.0 - sigma)), 0.0) * scale).astype(BF16)
        attended = dot(jnp.concatenate([value[m] for m in at], axis=1), now)
        inv_rms = lax.rsqrt(jnp.sum(attended * attended, axis=0, keepdims=True) * (1.0 / HD) + 1.0)
        norm = attended * inv_rms
        normed[n] = norm
        ahead[n] = inv_rms * gain * gate[n].astype(F32)
        fac[n, 0] = gain * norm * fac[n, 0]
        return carry

    lax.fori_loop(0, count, attend, 0, unroll=2)

    def back_copy(src, landing, send, recv, d):
        n = source(d)
        return remote(src.at[n], landing.at[c], send.at[d], recv.at[d], (s, n))

    def back_arrival(src, landing, send, recv, d):
        h = to(d)
        return remote(src.at[h], landing.at[h], send.at[d], recv.at[d], (s, h))

    def head(d):
        n = source(d)
        at = [jnp.maximum(b, 0) for b in slots(n)]
        cot_n = cotin[n].astype(F32)
        norm = normed[n]
        steep = cot_n * ahead[n]
        mean = jnp.sum(steep * norm, axis=0, keepdims=True) * (1.0 / HD)
        ga = (steep - norm * mean).astype(BF16)
        gw = dot(jnp.concatenate([valuet[m] for m in at], axis=0), ga)
        gs = (gw * slope[n].astype(F32)).astype(BF16)
        gq = dot(jnp.concatenate([key[m] for m in at], axis=1), gs)
        gpa[n, :HD] = (cot_n * fac[n, 0]).astype(BF16)
        gpa[n, HD:] = (gq * fac[n, 1]).astype(BF16)
        gvt[n] = ntdot(ga, weight[n])
        gkt[n] = ntdot(query[n], gs)

    group = 2
    for g in range(0, count, group):
        for d in near[g : g + group]:
            if d:
                cot_arrival(d).wait_recv()
            else:

                @pl.when(jnp.logical_not(first))
                def _(d=d):
                    cot_arrival(d).wait_recv()

        for d in near[g : g + group]:
            head(d)
        for d in near[g : g + group]:
            if d:
                back_copy(gpa, gain_a, as_, ar, d).start()
    gain_a[c] = gpa[c]

    def seg_step(i, carry):
        run_v, run_k = carry
        n = plan_ref[3, i]
        keep = plan_ref[5, i].astype(F32)
        run_v = run_v * keep + gvt[n, :, 2 * BLOCK :]
        run_k = run_k * keep + gkt[n, :, 2 * BLOCK :]
        segv[i] = run_v
        segk[i] = run_k
        return run_v, run_k

    zero = jnp.zeros((HD, BLOCK), F32)
    lax.fori_loop(0, count, seg_step, (zero, zero), unroll=2)

    def finalise(d):
        m = source(d)
        later = lax.rem(m + 1, count)
        last = plan_ref[4, m]
        has = plan_ref[6, m].astype(F32)
        gv = gvt[m, :, :BLOCK] + gvt[later, :, BLOCK : 2 * BLOCK] + segv[last] * has
        gk = gkt[m, :, :BLOCK] + gkt[later, :, BLOCK : 2 * BLOCK] + segk[last] * has
        gpb[m, :HD] = (gv * fac[m, 2]).astype(BF16)
        gpb[m, HD:] = (gk * fac[m, 3]).astype(BF16)

    for d in far:
        finalise(d)
        back_copy(gpb, gain_b, bs, br, d).start()
    finalise(0)
    gain_b[c] = gpb[c]

    norm_factor = float(count * BLOCK) ** (-0.5)

    def weight_grad():
        for d in far[::-1]:
            x_arrival(d).wait_recv()
        whole = xall[...].reshape(count * BLOCK, width)
        for src, base in ((gpa, 0), (gpb, HD)):
            part = dot(jnp.concatenate([src[n] for n in range(count)], axis=1), whole) * norm_factor
            dw_ref[base : base + HD] = part[:HD]
            dw_ref[base + 2 * HD : base + 3 * HD] = part[HD:]

    def half_weights(parts, span):
        return jnp.concatenate([wi[h, p, :, span] for h in range(count) for p in parts], axis=0)

    for d in near[1:]:
        back_arrival(gpa, gain_a, as_, ar, d).wait_recv()
    left = gain_a[...].reshape(count * BLOCK, BLOCK)

    @pl.when(jnp.logical_not(first))
    def _():
        remote(sgsend, upbuf, us, ur, (s, c)).wait_recv()
        wo_push.wait_send()
    acc[...] = upbuf[...].astype(F32) + tdot(left, half_weights((0, 2), slice(None)))

    @pl.when(s == 0)
    def _():
        weight_grad()

    @pl.when(s > 0)
    def _():
        remote(wo_ref, wo_next, ws, wr, (s, c)).wait_recv()

    for d in near[1:]:
        back_arrival(gpb, gain_b, bs, br, d).wait_recv()
    left = gain_b[...].reshape(count * BLOCK, BLOCK)
    cols = width // CHUNKS
    for i in range(CHUNKS):
        span = slice(i * cols, (i + 1) * cols)
        part = (acc[:, span] + tdot(left, half_weights((1, 3), span))).astype(BF16)
        sgsend[:, span] = part
        sg_ref[:, span] = part

    up_push = remote(sgsend, upbuf, us, ur, (before, c))

    @pl.when(s > 0)
    def _():
        set_cot(cotsend, dot(sgsend[...], wo_next[...]))
        for d in near:
            cot_copy(d).start()
        up_push.start()

    @pl.when(second)
    def _():
        pl.semaphore_signal(go, inc=1, device_id=(after, c), device_id_type=MESH)

    @pl.when(first)
    def _():
        pl.semaphore_wait(go, 1)

    @pl.when(late)
    def _():
        for d in far:
            x_copy(d).start()

    @pl.when(s > 0)
    def _():
        weight_grad()

    @pl.when(first)
    def _():
        for d in far:
            first_copy(d).wait_send()

    for d in far:
        p_copy(to(d)).wait_send()
        back_copy(gpa, gain_a, as_, ar, d).wait_send()
        back_copy(gpb, gain_b, bs, br, d).wait_send()
        x_copy(d).wait_send()

    @pl.when(s > 0)
    def _():
        for d in far + [0]:
            cot_copy(d).wait_send()
        up_push.wait_send()


def per_device(key_blocks, ranker, section_inputs, output_grad, input_proj, output_proj, norm_gain):
    count = lax.axis_size("ctx")
    x = section_inputs[0, 0]
    width = x.shape[1]
    blocks = key_blocks[0]
    gain = norm_gain[0].reshape(count, 1, HD)
    ranks = ranker[0].reshape(count, 1, BLOCK)
    plan = segment_plan(blocks)
    vmem = pl.BlockSpec(memory_space=pltpu.VMEM)
    smem = pl.BlockSpec(memory_space=pltpu.SMEM)
    hbm = pl.BlockSpec(memory_space=pl.ANY)
    dma = pltpu.SemaphoreType.DMA
    full = 3 * BLOCK

    def half(*shape):
        return pltpu.VMEM(shape, BF16)

    def single(*shape):
        return pltpu.VMEM(shape, F32)

    sg, dw = pl.pallas_call(
        kernel,
        out_shape=(
            jax.ShapeDtypeStruct((BLOCK, width), BF16),
            jax.ShapeDtypeStruct((4 * HD, width), F32),
        ),
        in_specs=[smem, vmem, vmem, vmem, hbm, hbm, hbm],
        out_specs=(vmem, vmem),
        scratch_shapes=[
            half(BLOCK, width),
            half(width, BLOCK),
            half(count, 4, HD, width),
            half(width, width),
            half(width, width),
            half(count, 4 * HD, BLOCK),
            half(count, 4 * HD, BLOCK),
            half(count, BLOCK, width),
            half(count, HD, BLOCK),
            half(count, HD, BLOCK),
            half(count, HD, BLOCK),
            half(count, HD, BLOCK),
            half(count, BLOCK, HD),
            half(count, BLOCK, HD),
            half(count, full, BLOCK),
            half(count, full, BLOCK),
            single(count, HD, BLOCK),
            single(count, HD, BLOCK),
            single(count, 4, HD, BLOCK),
            single(count, BLOCK, BLOCK),
            half(BLOCK, width),
            half(BLOCK, width),
            half(count, HD, BLOCK),
            half(count, HD, BLOCK),
            half(count, HD, BLOCK),
            half(count, 2 * HD, BLOCK),
            half(count, 2 * HD, BLOCK),
            half(count, 2 * HD, BLOCK),
            half(count, 2 * HD, BLOCK),
            single(count, HD, full),
            single(count, HD, full),
            single(count, HD, BLOCK),
            single(count, HD, BLOCK),
            single(BLOCK, width),
            dma,
            dma((CHUNKS,)),
            dma,
        ]
        + [dma((count,)) for _ in range(11)]
        + [dma for _ in range(4)]
        + [pltpu.SemaphoreType.REGULAR],
        compiler_params=pltpu.CompilerParams(
            collective_id=0, has_side_effects=True, vmem_limit_bytes=58 * 1024 * 1024
        ),
        cost_estimate=pl.CostEstimate(flops=5 * 10**9, bytes_accessed=20 * 10**6, transcendentals=0),
    )(
        plan, output_grad[0], gain, ranks,
        x, input_proj[0].reshape(count, 4, HD, width), output_proj[0],
    )
    return sg[None, None], dw[None]


def solution(mesh):
    placed = (
        P(),
        P(),
        P("pipe", None, "ctx", None),
        P(None, "ctx", None),
        P("pipe", None, None),
        P("pipe", None, None),
        P("pipe", None),
    )
    return jax.shard_map(
        per_device,
        mesh=mesh,
        in_specs=placed,
        out_specs=(P("pipe", None, "ctx", None), P("pipe", "ctx", None)),
        check_vma=False,
    )
```

```python
import math

import jax
import jax.numpy as jnp
from jax import lax
from jax.experimental import pallas as pl
from jax.experimental.pallas import tpu as pltpu
from jax.sharding import PartitionSpec as P

BLOCK = 128
HD = 64
CHUNKS = 4
MESH = pl.DeviceIdType.MESH
F32 = jnp.float32
BF16 = jnp.bfloat16


def segment_plan(blocks):
    third = blocks[:, 2]
    count = third.shape[0]
    ids = jnp.arange(count, dtype=jnp.int32)
    before = (third[None, :] < third[:, None]) | ((third[None, :] == third[:, None]) & (ids[None, :] < ids[:, None]))
    place = jnp.sum(before.astype(jnp.int32), axis=1)
    order = jnp.sum(jnp.where(place[None, :] == ids[:, None], ids[None, :], 0), axis=1)
    ordered = jnp.sum(jnp.where(place[None, :] == ids[:, None], third[None, :], 0), axis=1)
    keep = (ordered == jnp.concatenate([ordered[:1] - 1, ordered[:-1]])).astype(jnp.int32)
    upto = jnp.sum((third[None, :] <= ids[:, None]).astype(jnp.int32), axis=1)
    has = jnp.any(third[None, :] == ids[:, None], axis=1).astype(jnp.int32)
    last = jnp.maximum(upto - 1, 0)
    return jnp.concatenate([blocks.T, jnp.stack([order, last, keep, has])], axis=0)


def dot(left, right):
    return jnp.dot(left, right, preferred_element_type=F32)


def ntdot(left, right):
    return lax.dot_general(left, right, (((1,), (1,)), ((), ())), preferred_element_type=F32)


def tdot(left, right):
    return lax.dot_general(left, right, (((0,), (0,)), ((), ())), preferred_element_type=F32)


def kernel(
    plan_ref, up_ref, gain_ref, row_ref, x_ref, wi_ref, wo_ref,
    sg_ref, dw_ref,
    xv, xt, wi, wo_own, wo_next, psend, pin, xall, gate, query, key, value, keyt, valuet, weight, slope,
    ahead, normed, fac, col, upbuf, sgsend, cotfirst, cotsend, cotin, cotown, open_send, open_all, gpa, gpb, gain_a, gain_b, gvt, gkt, segv, segk, acc,
    xl, wil, wol, ps, pr, fs, cs, cr, as_, ar, bs, br, xs, xr, us, ur, ws, wr, os_, or_, gs_, gr, go,
):
    count, _, width = xall.shape
    side = math.isqrt(count)
    per_chunk = count // CHUNKS
    s = lax.axis_index("pipe")
    c = lax.axis_index("ctx")
    sections = lax.axis_size("pipe")
    first = s == sections - 1
    second = s == sections - 2
    late = first | second | (s == sections - 4)
    cy, cz = c // side, lax.rem(c, side)

    def to(d):
        return lax.rem(cy + d // side, side) * side + lax.rem(cz + d % side, side)

    def source(d):
        return lax.rem(cy + side - d // side, side) * side + lax.rem(cz + side - d % side, side)

    def distance(d):
        y, z = d // side, d % side
        return min(y, side - y) + min(z, side - z)

    near = sorted(range(count), key=distance)
    far = [d for d in near[::-1] if d]

    def remote(src, dst, send, recv, where):
        return pltpu.make_async_remote_copy(
            src_ref=src, dst_ref=dst, send_sem=send, recv_sem=recv, device_id=where, device_id_type=MESH
        )

    x_load = pltpu.make_async_copy(x_ref, xv, xl)
    wo_load = pltpu.make_async_copy(wo_ref, wo_own, wol)

    def wi_load(k):
        span = pl.ds(k * per_chunk, per_chunk)
        return pltpu.make_async_copy(wi_ref.at[span], wi.at[span], wil.at[k])

    def chunk_at(i):
        return lax.rem(c // per_chunk + i, CHUNKS)

    x_load.start()

    @pl.when(first)
    def _():
        wo_load.start()

    for i in range(CHUNKS):
        wi_load(chunk_at(i)).start()

    barrier = pltpu.get_barrier_semaphore()
    after, before = lax.rem(s + 1, sections), lax.rem(s + sections - 1, sections)
    pl.semaphore_signal(barrier, inc=1, device_id=(before, c), device_id_type=MESH)
    for d in range(1, count):
        pl.semaphore_signal(barrier, inc=1, device_id=(s, to(d)), device_id_type=MESH)
    for h in range(count):
        pl.semaphore_signal(barrier, inc=1, device_id=(after, h), device_id_type=MESH)
    def set_cot(held, cot):
        held[...] = cot.T.astype(BF16).reshape(count, HD, BLOCK)

    def spread(m, carry):
        col[m] = jnp.broadcast_to(row_ref[m].astype(F32), (BLOCK, BLOCK)).T
        return carry

    lax.fori_loop(0, count, spread, 0)

    x_load.wait()
    xt[...] = xv[...].T

    @pl.when(first)
    def _():
        wo_load.wait()
        set_cot(cotfirst, dot(up_ref[...], wo_own[...]))

    pl.semaphore_wait(barrier, 2 * count)

    wo_push = remote(wo_ref, wo_next, ws, wr, (after, c))

    @pl.when(jnp.logical_not(first))
    def _():
        wo_push.start()

    def first_copy(d):
        h = to(d)
        return remote(cotfirst.at[h], cotin.at[c], fs.at[d], cr.at[d], (s, h))

    def cot_copy(d):
        h = to(d)
        return remote(cotsend.at[h], cotin.at[c], cs.at[d], cr.at[d], (before, h))

    def cot_arrival(d):
        n = source(d)
        return remote(cotsend.at[n], cotin.at[n], cs.at[d], cr.at[d], (s, n))

    def p_copy(h):
        return remote(psend.at[h], pin.at[c], ps.at[h], pr.at[c], (s, h))

    def p_arrival(h):
        return remote(psend.at[h], pin.at[h], ps.at[h], pr.at[h], (s, h))


    def project(i, carry):
        k = chunk_at(i)
        span = pl.ds(k * per_chunk, per_chunk)
        wi_load(k).wait()
        rows = wi[span].reshape(per_chunk * 4 * HD, width)
        psend[span] = dot(rows, xt[...]).astype(BF16).reshape(per_chunk, 4 * HD, BLOCK)
        for j in range(per_chunk):
            h = k * per_chunk + j

            @pl.when(h != c)
            def _(h=h):
                p_copy(h).start()

        return carry

    @pl.when(second)
    def _():
        pl.semaphore_wait(go, 1)

    lax.fori_loop(0, CHUNKS, project, 0)
    pin[c] = psend[c]

    @pl.when(first)
    def _():
        for d in far:
            first_copy(d).start()
        cotin[c] = cotfirst[c]
        upbuf[...] = up_ref[...]

    def x_copy(d):
        h = to(d)
        return remote(xv, xall.at[c], xs.at[d], xr.at[d], (s, h))

    def x_arrival(d):
        n = source(d)
        return remote(xv, xall.at[n], xs.at[d], xr.at[d], (s, n))

    def activate(d):
        n = source(d)
        if d:
            p_arrival(n).wait_recv()
        pre = pin[n].astype(F32)
        sigma = jax.nn.sigmoid(pre)
        act = (pre * sigma).astype(BF16)
        slopes = sigma * (1.0 + pre * (1.0 - sigma))
        gate[n] = act[:HD]
        value[n] = act[HD : 2 * HD]
        query[n] = act[2 * HD : 3 * HD]
        key[n] = act[3 * HD :]
        valuet[n] = act[HD : 2 * HD].astype(F32).T.astype(BF16)
        keyt[n] = act[3 * HD :].astype(F32).T.astype(BF16)
        fac[n, 0] = slopes[:HD]
        fac[n, 1] = slopes[2 * HD : 3 * HD]
        fac[n, 2] = slopes[HD : 2 * HD]
        fac[n, 3] = slopes[3 * HD :]

    for d in near:
        activate(d)

    @pl.when(first)
    def _():
        pl.semaphore_signal(go, inc=1, device_id=(before, c), device_id_type=MESH)

    @pl.when(jnp.logical_not(late))
    def _():
        for d in far:
            x_copy(d).start()

    xall[c] = xv[...]
    scale = HD ** (-0.5)
    gain = jnp.broadcast_to(gain_ref[c], (BLOCK, HD)).T
    apart = lax.broadcasted_iota(jnp.int32, (BLOCK, BLOCK), 0) - lax.broadcasted_iota(jnp.int32, (BLOCK, BLOCK), 1)

    def slots(n):
        return [plan_ref[t, n] for t in range(3)]

    def attend(n, carry):
        listed = slots(n)
        at = [jnp.maximum(b, 0) for b in listed]
        scores = dot(jnp.concatenate([keyt[m] for m in at], axis=0), query[n]) * scale
        rank = row_ref[n].astype(F32)
        allowed = jnp.concatenate(
            [
                (apart <= (n - b) * BLOCK) & (col[m] == jnp.where(b >= 0, rank, -1.0))
                for b, m in zip(listed, at)
            ],
            axis=0,
        )
        sigma = jax.nn.sigmoid(scores)
        now = jnp.where(allowed, scores * sigma, 0.0).astype(BF16)
        weight[n] = now
        slope[n] = (jnp.where(allowed, sigma * (1.0 + scores * (1.0 - sigma)), 0.0) * scale).astype(BF16)
        attended = dot(jnp.concatenate([value[m] for m in at], axis=1), now)
        inv_rms = lax.rsqrt(jnp.sum(attended * attended, axis=0, keepdims=True) * (1.0 / HD) + 1.0)
        norm = attended * inv_rms
        normed[n] = norm
        ahead[n] = inv_rms * gain * gate[n].astype(F32)
        opening = gain * norm * fac[n, 0]
        fac[n, 0] = opening
        open_send[n] = opening.astype(BF16)
        return carry

    lax.fori_loop(0, count, attend, 0, unroll=2)

    def back_copy(src, landing, send, recv, d):
        n = source(d)
        return remote(src.at[n], landing.at[c], send.at[d], recv.at[d], (s, n))

    def query_copy(d):
        n = source(d)
        return remote(gpa.at[n, pl.ds(HD, HD)], gain_a.at[c], as_.at[d], ar.at[d], (s, n))

    def query_arrival(d):
        h = to(d)
        return remote(gpa.at[h, pl.ds(HD, HD)], gain_a.at[h], as_.at[d], ar.at[d], (s, h))

    def back_arrival(src, landing, send, recv, d):
        h = to(d)
        return remote(src.at[h], landing.at[h], send.at[d], recv.at[d], (s, h))

    for d in far:
        back_copy(open_send, open_all, gs_, gr, d).start()
    open_all[c] = open_send[c]

    def head(d):
        n = source(d)
        at = [jnp.maximum(b, 0) for b in slots(n)]
        cot_n = cotin[n].astype(F32)
        norm = normed[n]
        steep = cot_n * ahead[n]
        mean = jnp.sum(steep * norm, axis=0, keepdims=True) * (1.0 / HD)
        ga = (steep - norm * mean).astype(BF16)
        gw = dot(jnp.concatenate([valuet[m] for m in at], axis=0), ga)
        gs = (gw * slope[n].astype(F32)).astype(BF16)
        gq = dot(jnp.concatenate([key[m] for m in at], axis=1), gs)
        gpa[n, :HD] = (cot_n * fac[n, 0]).astype(BF16)
        gpa[n, HD:] = (gq * fac[n, 1]).astype(BF16)
        gvt[n] = ntdot(ga, weight[n])
        gkt[n] = ntdot(query[n], gs)

    group = 2
    for g in range(0, count, group):
        for d in near[g : g + group]:
            if d:
                cot_arrival(d).wait_recv()
            else:

                @pl.when(jnp.logical_not(first))
                def _(d=d):
                    cot_arrival(d).wait_recv()

        for d in near[g : g + group]:
            head(d)
        for d in near[g : g + group]:
            if d:
                query_copy(d).start()
    gain_a[c] = gpa[c, HD:]

    def seg_step(i, carry):
        run_v, run_k = carry
        n = plan_ref[3, i]
        keep = plan_ref[5, i].astype(F32)
        run_v = run_v * keep + gvt[n, :, 2 * BLOCK :]
        run_k = run_k * keep + gkt[n, :, 2 * BLOCK :]
        segv[i] = run_v
        segk[i] = run_k
        return run_v, run_k

    zero = jnp.zeros((HD, BLOCK), F32)
    lax.fori_loop(0, count, seg_step, (zero, zero), unroll=2)

    def finalise(d):
        m = source(d)
        later = lax.rem(m + 1, count)
        last = plan_ref[4, m]
        has = plan_ref[6, m].astype(F32)
        gv = gvt[m, :, :BLOCK] + gvt[later, :, BLOCK : 2 * BLOCK] + segv[last] * has
        gk = gkt[m, :, :BLOCK] + gkt[later, :, BLOCK : 2 * BLOCK] + segk[last] * has
        gpb[m, :HD] = (gv * fac[m, 2]).astype(BF16)
        gpb[m, HD:] = (gk * fac[m, 3]).astype(BF16)

    for d in far:
        finalise(d)
        back_copy(gpb, gain_b, bs, br, d).start()
    finalise(0)
    gain_b[c] = gpb[c]

    norm_factor = float(count * BLOCK) ** (-0.5)

    def weight_grad():
        for d in far[::-1]:
            x_arrival(d).wait_recv()
        whole = xall[...].reshape(count * BLOCK, width)
        for src, base in ((gpa, 0), (gpb, HD)):
            part = dot(jnp.concatenate([src[n] for n in range(count)], axis=1), whole) * norm_factor
            dw_ref[base : base + HD] = part[:HD]
            dw_ref[base + 2 * HD : base + 3 * HD] = part[HD:]

    def half_weights(parts, span):
        return jnp.concatenate([wi[h, p, :, span] for h in range(count) for p in parts], axis=0)

    own_push = remote(cotsend, cotown, os_, or_, (before, c))

    for d in near[1:]:
        back_arrival(open_send, open_all, gs_, gr, d).wait_recv()

    @pl.when(jnp.logical_not(first))
    def _():
        remote(sgsend, upbuf, us, ur, (s, c)).wait_recv()
        remote(cotsend, cotown, os_, or_, (s, c)).wait_recv()
        wo_push.wait_send()

    @pl.when(first)
    def _():
        cotown[...] = cotfirst[...]

    opened = (cotown[...].astype(F32) * open_all[...].astype(F32)).astype(BF16).reshape(count * HD, BLOCK)
    acc[...] = upbuf[...].astype(F32) + tdot(opened, half_weights((0,), slice(None)))
    for d in near[1:]:
        query_arrival(d).wait_recv()
    acc[...] += tdot(gain_a[...].reshape(count * HD, BLOCK), half_weights((2,), slice(None)))

    @pl.when(s == 0)
    def _():
        weight_grad()

    @pl.when(s > 0)
    def _():
        remote(wo_ref, wo_next, ws, wr, (s, c)).wait_recv()

    for d in near[1:]:
        back_arrival(gpb, gain_b, bs, br, d).wait_recv()
    left = gain_b[...].reshape(count * BLOCK, BLOCK)
    cols = width // CHUNKS
    for i in range(CHUNKS):
        span = slice(i * cols, (i + 1) * cols)
        part = (acc[:, span] + tdot(left, half_weights((1, 3), span))).astype(BF16)
        sgsend[:, span] = part
        sg_ref[:, span] = part

    up_push = remote(sgsend, upbuf, us, ur, (before, c))

    @pl.when(s > 0)
    def _():
        set_cot(cotsend, dot(sgsend[...], wo_next[...]))
        for d in near:
            cot_copy(d).start()
        up_push.start()
        own_push.start()

    @pl.when(second)
    def _():
        pl.semaphore_signal(go, inc=1, device_id=(after, c), device_id_type=MESH)

    @pl.when(first)
    def _():
        pl.semaphore_wait(go, 1)

    @pl.when(late)
    def _():
        for d in far:
            x_copy(d).start()

    @pl.when(s > 0)
    def _():
        weight_grad()

    @pl.when(first)
    def _():
        for d in far:
            first_copy(d).wait_send()

    for d in far:
        p_copy(to(d)).wait_send()
        query_copy(d).wait_send()
        back_copy(open_send, open_all, gs_, gr, d).wait_send()
        back_copy(gpb, gain_b, bs, br, d).wait_send()
        x_copy(d).wait_send()

    @pl.when(s > 0)
    def _():
        for d in far + [0]:
            cot_copy(d).wait_send()
        up_push.wait_send()
        own_push.wait_send()


def per_device(key_blocks, ranker, section_inputs, output_grad, input_proj, output_proj, norm_gain):
    count = lax.axis_size("ctx")
    x = section_inputs[0, 0]
    width = x.shape[1]
    blocks = key_blocks[0]
    gain = norm_gain[0].reshape(count, 1, HD)
    ranks = ranker[0].reshape(count, 1, BLOCK)
    plan = segment_plan(blocks)
    vmem = pl.BlockSpec(memory_space=pltpu.VMEM)
    smem = pl.BlockSpec(memory_space=pltpu.SMEM)
    hbm = pl.BlockSpec(memory_space=pl.ANY)
    dma = pltpu.SemaphoreType.DMA
    full = 3 * BLOCK

    def half(*shape):
        return pltpu.VMEM(shape, BF16)

    def single(*shape):
        return pltpu.VMEM(shape, F32)

    sg, dw = pl.pallas_call(
        kernel,
        out_shape=(
            jax.ShapeDtypeStruct((BLOCK, width), BF16),
            jax.ShapeDtypeStruct((4 * HD, width), F32),
        ),
        in_specs=[smem, vmem, vmem, vmem, hbm, hbm, hbm],
        out_specs=(vmem, vmem),
        scratch_shapes=[
            half(BLOCK, width),
            half(width, BLOCK),
            half(count, 4, HD, width),
            half(width, width),
            half(width, width),
            half(count, 4 * HD, BLOCK),
            half(count, 4 * HD, BLOCK),
            half(count, BLOCK, width),
            half(count, HD, BLOCK),
            half(count, HD, BLOCK),
            half(count, HD, BLOCK),
            half(count, HD, BLOCK),
            half(count, BLOCK, HD),
            half(count, BLOCK, HD),
            half(count, full, BLOCK),
            half(count, full, BLOCK),
            single(count, HD, BLOCK),
            single(count, HD, BLOCK),
            single(count, 4, HD, BLOCK),
            single(count, BLOCK, BLOCK),
            half(BLOCK, width),
            half(BLOCK, width),
            half(count, HD, BLOCK),
            half(count, HD, BLOCK),
            half(count, HD, BLOCK),
            half(count, HD, BLOCK),
            half(count, HD, BLOCK),
            half(count, HD, BLOCK),
            half(count, 2 * HD, BLOCK),
            half(count, 2 * HD, BLOCK),
            half(count, HD, BLOCK),
            half(count, 2 * HD, BLOCK),
            single(count, HD, full),
            single(count, HD, full),
            single(count, HD, BLOCK),
            single(count, HD, BLOCK),
            single(BLOCK, width),
            dma,
            dma((CHUNKS,)),
            dma,
        ]
        + [dma((count,)) for _ in range(11)]
        + [dma for _ in range(6)]
        + [dma((count,)) for _ in range(2)]
        + [pltpu.SemaphoreType.REGULAR],
        compiler_params=pltpu.CompilerParams(
            collective_id=0, has_side_effects=True, vmem_limit_bytes=58 * 1024 * 1024
        ),
        cost_estimate=pl.CostEstimate(flops=5 * 10**9, bytes_accessed=20 * 10**6, transcendentals=0),
    )(
        plan, output_grad[0], gain, ranks,
        x, input_proj[0].reshape(count, 4, HD, width), output_proj[0],
    )
    return sg[None, None], dw[None]


def solution(mesh):
    placed = (
        P(),
        P(),
        P("pipe", None, "ctx", None),
        P(None, "ctx", None),
        P("pipe", None, None),
        P("pipe", None, None),
        P("pipe", None),
    )
    return jax.shard_map(
        per_device,
        mesh=mesh,
        in_specs=placed,
        out_specs=(P("pipe", None, "ctx", None), P("pipe", "ctx", None)),
        check_vma=False,
    )
```

```python
import math

import jax
import jax.numpy as jnp
from jax import lax
from jax.experimental import pallas as pl
from jax.experimental.pallas import tpu as pltpu
from jax.sharding import PartitionSpec as P

BLOCK = 128
HD = 64
CHUNKS = 4
MESH = pl.DeviceIdType.MESH
F32 = jnp.float32
BF16 = jnp.bfloat16


def dot(left, right):
    return jnp.dot(left, right, preferred_element_type=F32)


def ntdot(left, right):
    return lax.dot_general(left, right, (((1,), (1,)), ((), ())), preferred_element_type=F32)


def tdot(left, right):
    return lax.dot_general(left, right, (((0,), (0,)), ((), ())), preferred_element_type=F32)


def kernel(
    blocks_ref, up_ref, gain_ref, row_ref, x_ref, wi_ref, wo_ref,
    sg_ref, dw_ref,
    xv, xt, wi, wo_own, wo_next, psend, pin, xall, gate, query, key, value, keyt, valuet, weight, slope,
    ahead, normed, fac, col, upbuf, sgsend, cotfirst, cotsend, cotin, cotown, open_send, open_all, gpa, gpb, gain_a, gain_b, gvt, gkt, segv, segk, acc,
    xl, wil, wol, ps, pr, fs, cs, cr, as_, ar, bs, br, xs, xr, us, ur, ws, wr, os_, or_, gs_, gr, go, chain,
):
    count, _, width = xall.shape
    side = math.isqrt(count)
    per_chunk = count // CHUNKS
    s = lax.axis_index("pipe")
    c = lax.axis_index("ctx")
    sections = lax.axis_size("pipe")
    first = s == sections - 1
    second = s == sections - 2
    late = first | second | (s == sections - 4)
    cy, cz = c // side, lax.rem(c, side)

    def to(d):
        return lax.rem(cy + d // side, side) * side + lax.rem(cz + d % side, side)

    def source(d):
        return lax.rem(cy + side - d // side, side) * side + lax.rem(cz + side - d % side, side)

    def distance(d):
        y, z = d // side, d % side
        return min(y, side - y) + min(z, side - z)

    near = sorted(range(count), key=distance)
    spiral = sorted(range(side), key=lambda v: min(v, side - v))
    far = [d for d in near[::-1] if d]

    def remote(src, dst, send, recv, where):
        return pltpu.make_async_remote_copy(
            src_ref=src, dst_ref=dst, send_sem=send, recv_sem=recv, device_id=where, device_id_type=MESH
        )

    x_load = pltpu.make_async_copy(x_ref, xv, xl)
    wo_load = pltpu.make_async_copy(wo_ref, wo_own, wol)

    def wi_load(k):
        span = pl.ds(k * per_chunk, per_chunk)
        return pltpu.make_async_copy(wi_ref.at[span], wi.at[span], wil.at[k])

    def chunk_at(i):
        return lax.rem(c // per_chunk + i, CHUNKS)

    x_load.start()

    @pl.when(first)
    def _():
        wo_load.start()

    for i in range(CHUNKS):
        wi_load(chunk_at(i)).start()

    barrier = pltpu.get_barrier_semaphore()
    after, before = lax.rem(s + 1, sections), lax.rem(s + sections - 1, sections)
    pl.semaphore_signal(barrier, inc=1, device_id=(before, c), device_id_type=MESH)
    for d in range(1, count):
        pl.semaphore_signal(barrier, inc=1, device_id=(s, to(d)), device_id_type=MESH)
    for h in range(count):
        pl.semaphore_signal(barrier, inc=1, device_id=(after, h), device_id_type=MESH)
    def set_cot(held, cot):
        held[...] = cot.T.astype(BF16).reshape(count, HD, BLOCK)

    def spread(m, carry):
        col[m] = jnp.broadcast_to(row_ref[m].astype(F32), (BLOCK, BLOCK)).T
        return carry

    lax.fori_loop(0, count, spread, 0)

    newest = [jnp.int32(-1)] * count
    for n in range(count):
        read = blocks_ref[n, 2]
        prior = jnp.int32(-1)
        for m in range(n):
            prior = jnp.where(read == m, newest[m], prior)
            newest[m] = jnp.where(read == m, n, newest[m])
        chain[0, n] = prior
    for m in range(count):
        chain[1, m] = newest[m]
    segv[...] = jnp.zeros_like(segv)
    segk[...] = jnp.zeros_like(segk)

    x_load.wait()
    xt[...] = xv[...].T

    @pl.when(first)
    def _():
        wo_load.wait()
        set_cot(cotfirst, dot(up_ref[...], wo_own[...]))

    pl.semaphore_wait(barrier, 2 * count)

    wo_push = remote(wo_ref, wo_next, ws, wr, (after, c))

    @pl.when(jnp.logical_not(first))
    def _():
        wo_push.start()

    def first_copy(d):
        h = to(d)
        return remote(cotfirst.at[h], cotin.at[c], fs.at[d], cr.at[d], (s, h))

    def cot_copy(d):
        h = to(d)
        return remote(cotsend.at[h], cotin.at[c], cs.at[d], cr.at[d], (before, h))

    def cot_arrival(d):
        n = source(d)
        return remote(cotsend.at[n], cotin.at[n], cs.at[d], cr.at[d], (s, n))

    def p_copy(h):
        return remote(psend.at[h], pin.at[c], ps.at[h], pr.at[c], (s, h))

    def p_arrival(h):
        return remote(psend.at[h], pin.at[h], ps.at[h], pr.at[h], (s, h))


    def project(i, carry):
        k = chunk_at(i)
        span = pl.ds(k * per_chunk, per_chunk)
        wi_load(k).wait()
        rows = wi[span].reshape(per_chunk * 4 * HD, width)
        psend[span] = dot(rows, xt[...]).astype(BF16).reshape(per_chunk, 4 * HD, BLOCK)
        for j in range(per_chunk):
            h = k * per_chunk + j

            @pl.when(h != c)
            def _(h=h):
                p_copy(h).start()

        return carry

    @pl.when(second)
    def _():
        pl.semaphore_wait(go, 1)

    lax.fori_loop(0, CHUNKS, project, 0)
    pin[c] = psend[c]

    @pl.when(first)
    def _():
        for d in far:
            first_copy(d).start()
        cotin[c] = cotfirst[c]
        upbuf[...] = up_ref[...]

    def x_copy(d):
        h = to(d)
        return remote(xv, xall.at[c], xs.at[d], xr.at[d], (s, h))

    def x_arrival(d):
        n = source(d)
        return remote(xv, xall.at[n], xs.at[d], xr.at[d], (s, n))

    def activate(d):
        n = source(d)
        if d:
            p_arrival(n).wait_recv()
        pre = pin[n].astype(F32)
        sigma = jax.nn.sigmoid(pre)
        act = (pre * sigma).astype(BF16)
        slopes = sigma * (1.0 + pre * (1.0 - sigma))
        gate[n] = act[:HD]
        value[n] = act[HD : 2 * HD]
        query[n] = act[2 * HD : 3 * HD]
        key[n] = act[3 * HD :]
        valuet[n] = act[HD : 2 * HD].astype(F32).T.astype(BF16)
        keyt[n] = act[3 * HD :].astype(F32).T.astype(BF16)
        fac[n, 0] = slopes[:HD]
        fac[n, 1] = slopes[2 * HD : 3 * HD]
        fac[n, 2] = slopes[HD : 2 * HD]
        fac[n, 3] = slopes[3 * HD :]

    for d in near:
        activate(d)

    @pl.when(first)
    def _():
        pl.semaphore_signal(go, inc=1, device_id=(before, c), device_id_type=MESH)

    @pl.when(jnp.logical_not(late))
    def _():
        for d in far:
            x_copy(d).start()

    xall[c] = xv[...]
    scale = HD ** (-0.5)
    gain = jnp.broadcast_to(gain_ref[c], (BLOCK, HD)).T
    apart = lax.broadcasted_iota(jnp.int32, (BLOCK, BLOCK), 0) - lax.broadcasted_iota(jnp.int32, (BLOCK, BLOCK), 1)

    def slots(n):
        return [blocks_ref[n, t] for t in range(3)]

    def attend(n, carry):
        listed = slots(n)
        at = [jnp.maximum(b, 0) for b in listed]
        scores = dot(jnp.concatenate([keyt[m] for m in at], axis=0), query[n]) * scale
        rank = row_ref[n].astype(F32)
        allowed = jnp.concatenate(
            [
                (apart <= (n - b) * BLOCK) & (col[m] == jnp.where(b >= 0, rank, -1.0))
                for b, m in zip(listed, at)
            ],
            axis=0,
        )
        sigma = jax.nn.sigmoid(scores)
        now = jnp.where(allowed, scores * sigma, 0.0).astype(BF16)
        weight[n] = now
        slope[n] = (jnp.where(allowed, sigma * (1.0 + scores * (1.0 - sigma)), 0.0) * scale).astype(BF16)
        attended = dot(jnp.concatenate([value[m] for m in at], axis=1), now)
        inv_rms = lax.rsqrt(jnp.sum(attended * attended, axis=0, keepdims=True) * (1.0 / HD) + 1.0)
        norm = attended * inv_rms
        normed[n] = norm
        ahead[n] = inv_rms * gain * gate[n].astype(F32)
        opening = gain * norm * fac[n, 0]
        fac[n, 0] = opening
        open_send[n] = opening.astype(BF16)
        return carry

    lax.fori_loop(0, count, attend, 0, unroll=2)

    def back_copy(src, landing, send, recv, d):
        n = source(d)
        return remote(src.at[n], landing.at[c], send.at[d], recv.at[d], (s, n))

    def query_copy(d):
        n = source(d)
        return remote(gpa.at[n, pl.ds(HD, HD)], gain_a.at[c], as_.at[d], ar.at[d], (s, n))

    def query_arrival(d):
        h = to(d)
        return remote(gpa.at[h, pl.ds(HD, HD)], gain_a.at[h], as_.at[d], ar.at[d], (s, h))

    def back_arrival(src, landing, send, recv, d):
        h = to(d)
        return remote(src.at[h], landing.at[h], send.at[d], recv.at[d], (s, h))

    for d in far:
        back_copy(open_send, open_all, gs_, gr, d).start()
    open_all[c] = open_send[c]

    def head(d):
        n = source(d)
        at = [jnp.maximum(b, 0) for b in slots(n)]
        cot_n = cotin[n].astype(F32)
        norm = normed[n]
        steep = cot_n * ahead[n]
        mean = jnp.sum(steep * norm, axis=0, keepdims=True) * (1.0 / HD)
        ga = (steep - norm * mean).astype(BF16)
        gw = dot(jnp.concatenate([valuet[m] for m in at], axis=0), ga)
        gs = (gw * slope[n].astype(F32)).astype(BF16)
        gq = dot(jnp.concatenate([key[m] for m in at], axis=1), gs)
        gpa[n, :HD] = (cot_n * fac[n, 0]).astype(BF16)
        gpa[n, HD:] = (gq * fac[n, 1]).astype(BF16)
        gvt[n] = ntdot(ga, weight[n])
        gkt[n] = ntdot(query[n], gs)

    group = 2
    for g in range(0, count, group):
        for d in near[g : g + group]:
            if d:
                cot_arrival(d).wait_recv()
            else:

                @pl.when(jnp.logical_not(first))
                def _(d=d):
                    cot_arrival(d).wait_recv()

        for d in near[g : g + group]:
            head(d)
        for d in near[g : g + group]:
            if d:
                query_copy(d).start()
    gain_a[c] = gpa[c, HD:]

    def seg_step(n, carry):
        prior = chain[0, n]
        back = jnp.maximum(prior, 0)
        keep = (prior >= 0).astype(F32)
        segv[n] = segv[back] * keep + gvt[n, :, 2 * BLOCK :]
        segk[n] = segk[back] * keep + gkt[n, :, 2 * BLOCK :]
        return carry

    lax.fori_loop(0, count, seg_step, 0, unroll=2)

    def finalise(d):
        m = source(d)
        later = lax.rem(m + 1, count)
        newest = chain[1, m]
        last = jnp.maximum(newest, 0)
        has = (newest >= 0).astype(F32)
        gv = gvt[m, :, :BLOCK] + gvt[later, :, BLOCK : 2 * BLOCK] + segv[last] * has
        gk = gkt[m, :, :BLOCK] + gkt[later, :, BLOCK : 2 * BLOCK] + segk[last] * has
        gpb[m, :HD] = (gv * fac[m, 2]).astype(BF16)
        gpb[m, HD:] = (gk * fac[m, 3]).astype(BF16)

    for d in far:
        finalise(d)
        back_copy(gpb, gain_b, bs, br, d).start()
    finalise(0)
    gain_b[c] = gpb[c]

    norm_factor = float(count * BLOCK) ** (-0.5)

    def weight_grad():
        for d in far[::-1]:
            x_arrival(d).wait_recv()
        whole = xall[...].reshape(count * BLOCK, width)
        for src, base in ((gpa, 0), (gpb, HD)):
            part = dot(jnp.concatenate([src[n] for n in range(count)], axis=1), whole) * norm_factor
            dw_ref[base : base + HD] = part[:HD]
            dw_ref[base + 2 * HD : base + 3 * HD] = part[HD:]

    def half_weights(parts, span):
        return jnp.concatenate([wi[h, p, :, span] for h in range(count) for p in parts], axis=0)

    own_push = remote(cotsend, cotown, os_, or_, (before, c))

    for d in near[1:]:
        back_arrival(open_send, open_all, gs_, gr, d).wait_recv()

    @pl.when(jnp.logical_not(first))
    def _():
        remote(sgsend, upbuf, us, ur, (s, c)).wait_recv()
        remote(cotsend, cotown, os_, or_, (s, c)).wait_recv()
        wo_push.wait_send()

    @pl.when(first)
    def _():
        cotown[...] = cotfirst[...]

    opened = (cotown[...].astype(F32) * open_all[...].astype(F32)).astype(BF16).reshape(count * HD, BLOCK)
    acc[...] = upbuf[...].astype(F32) + tdot(opened, half_weights((0,), slice(None)))
    for d in near[1:]:
        query_arrival(d).wait_recv()
    acc[...] += tdot(gain_a[...].reshape(count * HD, BLOCK), half_weights((2,), slice(None)))

    @pl.when(s == 0)
    def _():
        weight_grad()

    @pl.when(s > 0)
    def _():
        remote(wo_ref, wo_next, ws, wr, (s, c)).wait_recv()

    for d in near[1:]:
        back_arrival(gpb, gain_b, bs, br, d).wait_recv()
    left = gain_b[...].reshape(count * BLOCK, BLOCK)
    cols = width // CHUNKS
    for i in range(CHUNKS):
        span = slice(i * cols, (i + 1) * cols)
        part = (acc[:, span] + tdot(left, half_weights((1, 3), span))).astype(BF16)
        sgsend[:, span] = part
        sg_ref[:, span] = part

    up_push = remote(sgsend, upbuf, us, ur, (before, c))

    @pl.when(s > 0)
    def _():
        for dy in spiral:
            k = lax.rem(cy + dy, side)
            cols = pl.ds(pl.multiple_of(k * side * HD, side * HD), side * HD)
            part = dot(sgsend[...], wo_next[:, cols])
            cotsend[pl.ds(k * side, side)] = part.T.astype(BF16).reshape(side, HD, BLOCK)
            for dz in spiral:
                cot_copy(dy * side + dz).start()
        up_push.start()
        own_push.start()

    @pl.when(second)
    def _():
        pl.semaphore_signal(go, inc=1, device_id=(after, c), device_id_type=MESH)

    @pl.when(first)
    def _():
        pl.semaphore_wait(go, 1)

    @pl.when(late)
    def _():
        for d in far:
            x_copy(d).start()

    @pl.when(s > 0)
    def _():
        weight_grad()

    @pl.when(first)
    def _():
        for d in far:
            first_copy(d).wait_send()

    for d in far:
        p_copy(to(d)).wait_send()
        query_copy(d).wait_send()
        back_copy(open_send, open_all, gs_, gr, d).wait_send()
        back_copy(gpb, gain_b, bs, br, d).wait_send()
        x_copy(d).wait_send()

    @pl.when(s > 0)
    def _():
        for d in far + [0]:
            cot_copy(d).wait_send()
        up_push.wait_send()
        own_push.wait_send()


def per_device(key_blocks, ranker, section_inputs, output_grad, input_proj, output_proj, norm_gain):
    count = lax.axis_size("ctx")
    x = section_inputs[0, 0]
    width = x.shape[1]
    blocks = key_blocks[0]
    gain = norm_gain[0].reshape(count, 1, HD)
    ranks = ranker[0].reshape(count, 1, BLOCK)
    vmem = pl.BlockSpec(memory_space=pltpu.VMEM)
    smem = pl.BlockSpec(memory_space=pltpu.SMEM)
    hbm = pl.BlockSpec(memory_space=pl.ANY)
    dma = pltpu.SemaphoreType.DMA
    full = 3 * BLOCK

    def half(*shape):
        return pltpu.VMEM(shape, BF16)

    def single(*shape):
        return pltpu.VMEM(shape, F32)

    sg, dw = pl.pallas_call(
        kernel,
        out_shape=(
            jax.ShapeDtypeStruct((BLOCK, width), BF16),
            jax.ShapeDtypeStruct((4 * HD, width), F32),
        ),
        in_specs=[smem, vmem, vmem, vmem, hbm, hbm, hbm],
        out_specs=(vmem, vmem),
        scratch_shapes=[
            half(BLOCK, width),
            half(width, BLOCK),
            half(count, 4, HD, width),
            half(width, width),
            half(width, width),
            half(count, 4 * HD, BLOCK),
            half(count, 4 * HD, BLOCK),
            half(count, BLOCK, width),
            half(count, HD, BLOCK),
            half(count, HD, BLOCK),
            half(count, HD, BLOCK),
            half(count, HD, BLOCK),
            half(count, BLOCK, HD),
            half(count, BLOCK, HD),
            half(count, full, BLOCK),
            half(count, full, BLOCK),
            single(count, HD, BLOCK),
            single(count, HD, BLOCK),
            single(count, 4, HD, BLOCK),
            single(count, BLOCK, BLOCK),
            half(BLOCK, width),
            half(BLOCK, width),
            half(count, HD, BLOCK),
            half(count, HD, BLOCK),
            half(count, HD, BLOCK),
            half(count, HD, BLOCK),
            half(count, HD, BLOCK),
            half(count, HD, BLOCK),
            half(count, 2 * HD, BLOCK),
            half(count, 2 * HD, BLOCK),
            half(count, HD, BLOCK),
            half(count, 2 * HD, BLOCK),
            single(count, HD, full),
            single(count, HD, full),
            single(count, HD, BLOCK),
            single(count, HD, BLOCK),
            single(BLOCK, width),
            dma,
            dma((CHUNKS,)),
            dma,
        ]
        + [dma((count,)) for _ in range(11)]
        + [dma for _ in range(6)]
        + [dma((count,)) for _ in range(2)]
        + [pltpu.SemaphoreType.REGULAR, pltpu.SMEM((2, count), jnp.int32)],
        compiler_params=pltpu.CompilerParams(
            collective_id=0, has_side_effects=True, vmem_limit_bytes=58 * 1024 * 1024
        ),
        cost_estimate=pl.CostEstimate(flops=5 * 10**9, bytes_accessed=20 * 10**6, transcendentals=0),
    )(
        blocks, output_grad[0], gain, ranks,
        x, input_proj[0].reshape(count, 4, HD, width), output_proj[0],
    )
    return sg[None, None], dw[None]


def solution(mesh):
    placed = (
        P(),
        P(),
        P("pipe", None, "ctx", None),
        P(None, "ctx", None),
        P("pipe", None, None),
        P("pipe", None, None),
        P("pipe", None),
    )
    return jax.shard_map(
        per_device,
        mesh=mesh,
        in_specs=placed,
        out_specs=(P("pipe", None, "ctx", None), P("pipe", "ctx", None)),
        check_vma=False,
    )
```

```python
import math

import jax
import jax.numpy as jnp
from jax import lax
from jax.experimental import pallas as pl
from jax.experimental.pallas import tpu as pltpu
from jax.sharding import PartitionSpec as P

BLOCK = 128
HD = 64
CHUNKS = 4
MESH = pl.DeviceIdType.MESH
F32 = jnp.float32
BF16 = jnp.bfloat16


def dot(left, right):
    return jnp.dot(left, right, preferred_element_type=F32)


def ntdot(left, right):
    return lax.dot_general(left, right, (((1,), (1,)), ((), ())), preferred_element_type=F32)


def tdot(left, right):
    return lax.dot_general(left, right, (((0,), (0,)), ((), ())), preferred_element_type=F32)


def kernel(
    blocks_ref, up_ref, gain_ref, row_ref, x_ref, wi_ref, wo_ref,
    sg_ref, dw_ref,
    xv, xt, wi, wo_own, wo_next, psend, pin, xall, gate, query, key, value, keyt, valuet, weight, slope,
    ahead, normed, fac, col, upbuf, sgsend, cotfirst, cotsend, cotin, cotown, open_send, open_all, gpa, gpb, gain_a, gain_b, gvt, gkt, segv, segk, acc,
    xl, wil, wol, ps, pr, fs, cs, cr, as_, ar, bs, br, xs, xr, us, ur, ws, wr, os_, or_, gs_, gr, go, chain,
):
    count, _, width = xall.shape
    side = math.isqrt(count)
    per_chunk = count // CHUNKS
    s = lax.axis_index("pipe")
    c = lax.axis_index("ctx")
    sections = lax.axis_size("pipe")
    first = s == sections - 1
    second = s == sections - 2
    late = first | second | (s == sections - 4)
    cy, cz = c // side, lax.rem(c, side)

    def to(d):
        return lax.rem(cy + d // side, side) * side + lax.rem(cz + d % side, side)

    def source(d):
        return lax.rem(cy + side - d // side, side) * side + lax.rem(cz + side - d % side, side)

    def distance(d):
        y, z = d // side, d % side
        return min(y, side - y) + min(z, side - z)

    near = sorted(range(count), key=distance)
    spiral = sorted(range(side), key=lambda v: min(v, side - v))
    far = [d for d in near[::-1] if d]

    def remote(src, dst, send, recv, where):
        return pltpu.make_async_remote_copy(
            src_ref=src, dst_ref=dst, send_sem=send, recv_sem=recv, device_id=where, device_id_type=MESH
        )

    x_load = pltpu.make_async_copy(x_ref, xv, xl)
    wo_load = pltpu.make_async_copy(wo_ref, wo_own, wol)

    def wi_load(k):
        span = pl.ds(k * per_chunk, per_chunk)
        return pltpu.make_async_copy(wi_ref.at[span], wi.at[span], wil.at[k])

    def chunk_at(i):
        return lax.rem(c // per_chunk + i, CHUNKS)

    x_load.start()

    @pl.when(first)
    def _():
        wo_load.start()

    for i in range(CHUNKS):
        wi_load(chunk_at(i)).start()

    barrier = pltpu.get_barrier_semaphore()
    after, before = lax.rem(s + 1, sections), lax.rem(s + sections - 1, sections)
    pl.semaphore_signal(barrier, inc=1, device_id=(before, c), device_id_type=MESH)
    for d in range(1, count):
        pl.semaphore_signal(barrier, inc=1, device_id=(s, to(d)), device_id_type=MESH)
    for h in range(count):
        pl.semaphore_signal(barrier, inc=1, device_id=(after, h), device_id_type=MESH)
    def set_cot(held, cot):
        held[...] = cot.T.astype(BF16).reshape(count, HD, BLOCK)

    def spread(m, carry):
        col[m] = jnp.broadcast_to(row_ref[m].astype(F32), (BLOCK, BLOCK)).T
        return carry

    lax.fori_loop(0, count, spread, 0)

    newest = [jnp.int32(-1)] * count
    for n in range(count):
        read = blocks_ref[n, 2]
        prior = jnp.int32(-1)
        for m in range(n):
            prior = jnp.where(read == m, newest[m], prior)
            newest[m] = jnp.where(read == m, n, newest[m])
        chain[0, n] = prior
    for m in range(count):
        chain[1, m] = newest[m]
    segv[...] = jnp.zeros_like(segv)
    segk[...] = jnp.zeros_like(segk)

    x_load.wait()
    xt[...] = xv[...].T

    @pl.when(first)
    def _():
        wo_load.wait()
        set_cot(cotfirst, dot(up_ref[...], wo_own[...]))

    pl.semaphore_wait(barrier, 2 * count)

    wo_push = remote(wo_ref, wo_next, ws, wr, (after, c))

    @pl.when(jnp.logical_not(first))
    def _():
        wo_push.start()

    def first_copy(d):
        h = to(d)
        return remote(cotfirst.at[h], cotin.at[c], fs.at[d], cr.at[d], (s, h))

    def cot_copy(d):
        h = to(d)
        return remote(cotsend.at[h], cotin.at[c], cs.at[d], cr.at[d], (before, h))

    def cot_arrival(d):
        n = source(d)
        return remote(cotsend.at[n], cotin.at[n], cs.at[d], cr.at[d], (s, n))

    def p_copy(h):
        return remote(psend.at[h], pin.at[c], ps.at[h], pr.at[c], (s, h))

    def p_arrival(h):
        return remote(psend.at[h], pin.at[h], ps.at[h], pr.at[h], (s, h))


    def project(i, carry):
        k = chunk_at(i)
        span = pl.ds(k * per_chunk, per_chunk)
        wi_load(k).wait()
        rows = wi[span].reshape(per_chunk * 4 * HD, width)
        psend[span] = dot(rows, xt[...]).astype(BF16).reshape(per_chunk, 4 * HD, BLOCK)
        for j in range(per_chunk):
            h = k * per_chunk + j

            @pl.when(h != c)
            def _(h=h):
                p_copy(h).start()

        return carry

    @pl.when(second)
    def _():
        pl.semaphore_wait(go, 1)

    lax.fori_loop(0, CHUNKS, project, 0)
    pin[c] = psend[c]

    @pl.when(first)
    def _():
        for d in far:
            first_copy(d).start()
        cotin[c] = cotfirst[c]
        upbuf[...] = up_ref[...]

    def x_copy(d):
        h = to(d)
        return remote(xv, xall.at[c], xs.at[d], xr.at[d], (s, h))

    def x_arrival(d):
        n = source(d)
        return remote(xv, xall.at[n], xs.at[d], xr.at[d], (s, n))

    def activate(d):
        n = source(d)
        if d:
            p_arrival(n).wait_recv()
        pre = pin[n].astype(F32)
        sigma = jax.nn.sigmoid(pre)
        act = (pre * sigma).astype(BF16)
        slopes = sigma * (1.0 + pre * (1.0 - sigma))
        gate[n] = act[:HD]
        value[n] = act[HD : 2 * HD]
        query[n] = act[2 * HD : 3 * HD]
        key[n] = act[3 * HD :]
        valuet[n] = act[HD : 2 * HD].astype(F32).T.astype(BF16)
        keyt[n] = act[3 * HD :].astype(F32).T.astype(BF16)
        fac[n, 0] = slopes[:HD]
        fac[n, 1] = slopes[2 * HD : 3 * HD]
        fac[n, 2] = slopes[HD : 2 * HD]
        fac[n, 3] = slopes[3 * HD :]

    for d in near:
        activate(d)

    @pl.when(first)
    def _():
        pl.semaphore_signal(go, inc=1, device_id=(before, c), device_id_type=MESH)

    @pl.when(jnp.logical_not(late))
    def _():
        for d in far:
            x_copy(d).start()

    xall[c] = xv[...]
    scale = HD ** (-0.5)
    gain = jnp.broadcast_to(gain_ref[c], (BLOCK, HD)).T
    apart = lax.broadcasted_iota(jnp.int32, (BLOCK, BLOCK), 0) - lax.broadcasted_iota(jnp.int32, (BLOCK, BLOCK), 1)

    def slots(n):
        return [blocks_ref[n, t] for t in range(3)]

    def attend(n, carry):
        listed = slots(n)
        at = [jnp.maximum(b, 0) for b in listed]
        scores = dot(jnp.concatenate([keyt[m] for m in at], axis=0), query[n]) * scale
        rank = row_ref[n].astype(F32)
        allowed = jnp.concatenate(
            [
                (apart <= (n - b) * BLOCK) & (col[m] == jnp.where(b >= 0, rank, -1.0))
                for b, m in zip(listed, at)
            ],
            axis=0,
        )
        sigma = jax.nn.sigmoid(scores)
        now = jnp.where(allowed, scores * sigma, 0.0).astype(BF16)
        weight[n] = now.astype(F32).T.astype(BF16)
        slope[n] = (jnp.where(allowed, sigma * (1.0 + scores * (1.0 - sigma)), 0.0) * scale).astype(BF16)
        attended = dot(jnp.concatenate([value[m] for m in at], axis=1), now)
        inv_rms = lax.rsqrt(jnp.sum(attended * attended, axis=0, keepdims=True) * (1.0 / HD) + 1.0)
        norm = attended * inv_rms
        normed[n] = norm
        ahead[n] = inv_rms * gain * gate[n].astype(F32)
        opening = gain * norm * fac[n, 0]
        fac[n, 0] = opening
        open_send[n] = opening.astype(BF16)
        return carry

    lax.fori_loop(0, count, attend, 0, unroll=2)

    def back_copy(src, landing, send, recv, d):
        n = source(d)
        return remote(src.at[n], landing.at[c], send.at[d], recv.at[d], (s, n))

    def query_copy(d):
        n = source(d)
        return remote(gpa.at[n, pl.ds(HD, HD)], gain_a.at[c], as_.at[d], ar.at[d], (s, n))

    def query_arrival(d):
        h = to(d)
        return remote(gpa.at[h, pl.ds(HD, HD)], gain_a.at[h], as_.at[d], ar.at[d], (s, h))

    def back_arrival(src, landing, send, recv, d):
        h = to(d)
        return remote(src.at[h], landing.at[h], send.at[d], recv.at[d], (s, h))

    for d in far:
        back_copy(open_send, open_all, gs_, gr, d).start()
    open_all[c] = open_send[c]

    def head(d):
        n = source(d)
        at = [jnp.maximum(b, 0) for b in slots(n)]
        cot_n = cotin[n].astype(F32)
        norm = normed[n]
        steep = cot_n * ahead[n]
        mean = jnp.sum(steep * norm, axis=0, keepdims=True) * (1.0 / HD)
        ga = (steep - norm * mean).astype(BF16)
        gw = dot(jnp.concatenate([valuet[m] for m in at], axis=0), ga)
        gs = (gw * slope[n].astype(F32)).astype(BF16)
        gq = dot(jnp.concatenate([key[m] for m in at], axis=1), gs)
        gpa[n, :HD] = (cot_n * fac[n, 0]).astype(BF16)
        gpa[n, HD:] = (gq * fac[n, 1]).astype(BF16)
        gvt[n] = dot(ga, weight[n])
        gkt[n] = ntdot(query[n], gs)

    group = 2
    for g in range(0, count, group):
        for d in near[g : g + group]:
            if d:
                cot_arrival(d).wait_recv()
            else:

                @pl.when(jnp.logical_not(first))
                def _(d=d):
                    cot_arrival(d).wait_recv()

        for d in near[g : g + group]:
            head(d)
        for d in near[g : g + group]:
            if d:
                query_copy(d).start()
    gain_a[c] = gpa[c, HD:]

    def seg_step(n, carry):
        prior = chain[0, n]
        back = jnp.maximum(prior, 0)
        keep = (prior >= 0).astype(F32)
        segv[n] = segv[back] * keep + gvt[n, :, 2 * BLOCK :]
        segk[n] = segk[back] * keep + gkt[n, :, 2 * BLOCK :]
        return carry

    lax.fori_loop(0, count, seg_step, 0, unroll=2)

    def finalise(d):
        m = source(d)
        later = lax.rem(m + 1, count)
        newest = chain[1, m]
        last = jnp.maximum(newest, 0)
        has = (newest >= 0).astype(F32)
        gv = gvt[m, :, :BLOCK] + gvt[later, :, BLOCK : 2 * BLOCK] + segv[last] * has
        gk = gkt[m, :, :BLOCK] + gkt[later, :, BLOCK : 2 * BLOCK] + segk[last] * has
        gpb[m, :HD] = (gv * fac[m, 2]).astype(BF16)
        gpb[m, HD:] = (gk * fac[m, 3]).astype(BF16)

    for d in far:
        finalise(d)
        back_copy(gpb, gain_b, bs, br, d).start()
    finalise(0)
    gain_b[c] = gpb[c]

    norm_factor = float(count * BLOCK) ** (-0.5)

    def weight_grad():
        for d in far[::-1]:
            x_arrival(d).wait_recv()
        whole = xall[...].reshape(count * BLOCK, width)
        for src, base in ((gpa, 0), (gpb, HD)):
            part = dot(jnp.concatenate([src[n] for n in range(count)], axis=1), whole) * norm_factor
            dw_ref[base : base + HD] = part[:HD]
            dw_ref[base + 2 * HD : base + 3 * HD] = part[HD:]

    def half_weights(parts, span):
        return jnp.concatenate([wi[h, p, :, span] for h in range(count) for p in parts], axis=0)

    own_push = remote(cotsend, cotown, os_, or_, (before, c))

    for d in near[1:]:
        back_arrival(open_send, open_all, gs_, gr, d).wait_recv()

    @pl.when(jnp.logical_not(first))
    def _():
        remote(sgsend, upbuf, us, ur, (s, c)).wait_recv()
        remote(cotsend, cotown, os_, or_, (s, c)).wait_recv()
        wo_push.wait_send()

    @pl.when(first)
    def _():
        cotown[...] = cotfirst[...]

    opened = (cotown[...].astype(F32) * open_all[...].astype(F32)).astype(BF16).reshape(count * HD, BLOCK)
    acc[...] = upbuf[...].astype(F32) + tdot(opened, half_weights((0,), slice(None)))
    for d in near[1:]:
        query_arrival(d).wait_recv()
    acc[...] += tdot(gain_a[...].reshape(count * HD, BLOCK), half_weights((2,), slice(None)))

    @pl.when(s == 0)
    def _():
        weight_grad()

    @pl.when(s > 0)
    def _():
        remote(wo_ref, wo_next, ws, wr, (s, c)).wait_recv()

    for d in near[1:]:
        back_arrival(gpb, gain_b, bs, br, d).wait_recv()
    left = gain_b[...].reshape(count * BLOCK, BLOCK)
    cols = width // CHUNKS
    for i in range(CHUNKS):
        span = slice(i * cols, (i + 1) * cols)
        part = (acc[:, span] + tdot(left, half_weights((1, 3), span))).astype(BF16)
        sgsend[:, span] = part
        sg_ref[:, span] = part

    up_push = remote(sgsend, upbuf, us, ur, (before, c))

    @pl.when(s > 0)
    def _():
        for dy in spiral:
            k = lax.rem(cy + dy, side)
            cols = pl.ds(pl.multiple_of(k * side * HD, side * HD), side * HD)
            part = dot(sgsend[...], wo_next[:, cols])
            cotsend[pl.ds(k * side, side)] = part.T.astype(BF16).reshape(side, HD, BLOCK)
            for dz in spiral:
                cot_copy(dy * side + dz).start()
        up_push.start()
        own_push.start()

    @pl.when(second)
    def _():
        pl.semaphore_signal(go, inc=1, device_id=(after, c), device_id_type=MESH)

    @pl.when(first)
    def _():
        pl.semaphore_wait(go, 1)

    @pl.when(late)
    def _():
        for d in far:
            x_copy(d).start()

    @pl.when(s > 0)
    def _():
        weight_grad()

    @pl.when(first)
    def _():
        for d in far:
            first_copy(d).wait_send()

    for d in far:
        p_copy(to(d)).wait_send()
        query_copy(d).wait_send()
        back_copy(open_send, open_all, gs_, gr, d).wait_send()
        back_copy(gpb, gain_b, bs, br, d).wait_send()
        x_copy(d).wait_send()

    @pl.when(s > 0)
    def _():
        for d in far + [0]:
            cot_copy(d).wait_send()
        up_push.wait_send()
        own_push.wait_send()


def per_device(key_blocks, ranker, section_inputs, output_grad, input_proj, output_proj, norm_gain):
    count = lax.axis_size("ctx")
    x = section_inputs[0, 0]
    width = x.shape[1]
    blocks = key_blocks[0]
    gain = norm_gain[0].reshape(count, 1, HD)
    ranks = ranker[0].reshape(count, 1, BLOCK)
    vmem = pl.BlockSpec(memory_space=pltpu.VMEM)
    smem = pl.BlockSpec(memory_space=pltpu.SMEM)
    hbm = pl.BlockSpec(memory_space=pl.ANY)
    dma = pltpu.SemaphoreType.DMA
    full = 3 * BLOCK

    def half(*shape):
        return pltpu.VMEM(shape, BF16)

    def single(*shape):
        return pltpu.VMEM(shape, F32)

    sg, dw = pl.pallas_call(
        kernel,
        out_shape=(
            jax.ShapeDtypeStruct((BLOCK, width), BF16),
            jax.ShapeDtypeStruct((4 * HD, width), F32),
        ),
        in_specs=[smem, vmem, vmem, vmem, hbm, hbm, hbm],
        out_specs=(vmem, vmem),
        scratch_shapes=[
            half(BLOCK, width),
            half(width, BLOCK),
            half(count, 4, HD, width),
            half(width, width),
            half(width, width),
            half(count, 4 * HD, BLOCK),
            half(count, 4 * HD, BLOCK),
            half(count, BLOCK, width),
            half(count, HD, BLOCK),
            half(count, HD, BLOCK),
            half(count, HD, BLOCK),
            half(count, HD, BLOCK),
            half(count, BLOCK, HD),
            half(count, BLOCK, HD),
            half(count, BLOCK, full),
            half(count, full, BLOCK),
            single(count, HD, BLOCK),
            single(count, HD, BLOCK),
            single(count, 4, HD, BLOCK),
            single(count, BLOCK, BLOCK),
            half(BLOCK, width),
            half(BLOCK, width),
            half(count, HD, BLOCK),
            half(count, HD, BLOCK),
            half(count, HD, BLOCK),
            half(count, HD, BLOCK),
            half(count, HD, BLOCK),
            half(count, HD, BLOCK),
            half(count, 2 * HD, BLOCK),
            half(count, 2 * HD, BLOCK),
            half(count, HD, BLOCK),
            half(count, 2 * HD, BLOCK),
            single(count, HD, full),
            single(count, HD, full),
            single(count, HD, BLOCK),
            single(count, HD, BLOCK),
            single(BLOCK, width),
            dma,
            dma((CHUNKS,)),
            dma,
        ]
        + [dma((count,)) for _ in range(11)]
        + [dma for _ in range(6)]
        + [dma((count,)) for _ in range(2)]
        + [pltpu.SemaphoreType.REGULAR, pltpu.SMEM((2, count), jnp.int32)],
        compiler_params=pltpu.CompilerParams(
            collective_id=0, has_side_effects=True, vmem_limit_bytes=58 * 1024 * 1024
        ),
        cost_estimate=pl.CostEstimate(flops=5 * 10**9, bytes_accessed=20 * 10**6, transcendentals=0),
    )(
        blocks, output_grad[0], gain, ranks,
        x, input_proj[0].reshape(count, 4, HD, width), output_proj[0],
    )
    return sg[None, None], dw[None]


def solution(mesh):
    placed = (
        P(),
        P(),
        P("pipe", None, "ctx", None),
        P(None, "ctx", None),
        P("pipe", None, None),
        P("pipe", None, None),
        P("pipe", None),
    )
    return jax.shard_map(
        per_device,
        mesh=mesh,
        in_specs=placed,
        out_specs=(P("pipe", None, "ctx", None), P("pipe", "ctx", None)),
        check_vma=False,
    )
```

```python
import math

import jax
import jax.numpy as jnp
from jax import lax
from jax.experimental import pallas as pl
from jax.experimental.pallas import tpu as pltpu
from jax.sharding import PartitionSpec as P

BLOCK = 128
HD = 64
CHUNKS = 4
MESH = pl.DeviceIdType.MESH
F32 = jnp.float32
BF16 = jnp.bfloat16


def dot(left, right):
    return jnp.dot(left, right, preferred_element_type=F32)


def ntdot(left, right):
    return lax.dot_general(left, right, (((1,), (1,)), ((), ())), preferred_element_type=F32)


def tdot(left, right):
    return lax.dot_general(left, right, (((0,), (0,)), ((), ())), preferred_element_type=F32)


def kernel(
    blocks_ref, up_ref, gain_ref, row_ref, x_ref, wi_ref, wo_ref,
    sg_ref, dw_ref,
    xv, xt, wi, wo_own, wo_next, psend, pin, xall, gate, query, key, value, keyt, valuet, weight, slope,
    ahead, normed, fac, col, upbuf, sgsend, cotfirst, cotsend, cotin, cotown, open_send, open_all, gpa, gpb, gain_a, gain_b, gvt, gkt, segv, segk, acc,
    xl, wil, wol, ps, pr, fs, cs, cr, as_, ar, bs, br, xs, xr, us, ur, ws, wr, os_, or_, gs_, gr, go, chain,
):
    count, _, width = xall.shape
    side = math.isqrt(count)
    per_chunk = count // CHUNKS
    s = lax.axis_index("pipe")
    c = lax.axis_index("ctx")
    sections = lax.axis_size("pipe")
    first = s == sections - 1
    second = s == sections - 2
    late = first | second | (s == sections - 4)
    cy, cz = c // side, lax.rem(c, side)

    def to(d):
        return lax.rem(cy + d // side, side) * side + lax.rem(cz + d % side, side)

    def source(d):
        return lax.rem(cy + side - d // side, side) * side + lax.rem(cz + side - d % side, side)

    def distance(d):
        y, z = d // side, d % side
        return min(y, side - y) + min(z, side - z)

    near = sorted(range(count), key=distance)
    spiral = sorted(range(side), key=lambda v: min(v, side - v))
    far = [d for d in near[::-1] if d]

    def remote(src, dst, send, recv, where):
        return pltpu.make_async_remote_copy(
            src_ref=src, dst_ref=dst, send_sem=send, recv_sem=recv, device_id=where, device_id_type=MESH
        )

    x_load = pltpu.make_async_copy(x_ref, xv, xl)
    wo_load = pltpu.make_async_copy(wo_ref, wo_own, wol)

    def wi_load(k):
        span = pl.ds(k * per_chunk, per_chunk)
        return pltpu.make_async_copy(wi_ref.at[span], wi.at[span], wil.at[k])

    def chunk_at(i):
        return lax.rem(c // per_chunk + i, CHUNKS)

    x_load.start()

    @pl.when(first)
    def _():
        wo_load.start()

    for i in range(CHUNKS):
        wi_load(chunk_at(i)).start()

    barrier = pltpu.get_barrier_semaphore()
    after, before = lax.rem(s + 1, sections), lax.rem(s + sections - 1, sections)
    pl.semaphore_signal(barrier, inc=1, device_id=(before, c), device_id_type=MESH)
    for d in range(1, count):
        pl.semaphore_signal(barrier, inc=1, device_id=(s, to(d)), device_id_type=MESH)
    for h in range(count):
        pl.semaphore_signal(barrier, inc=1, device_id=(after, h), device_id_type=MESH)
    def set_cot(held, cot):
        held[...] = cot.T.astype(BF16).reshape(count, HD, BLOCK)

    def spread(m, carry):
        col[m] = jnp.broadcast_to(row_ref[m].astype(F32), (BLOCK, BLOCK)).T
        return carry

    lax.fori_loop(0, count, spread, 0)

    newest = [jnp.int32(-1)] * count
    for n in range(count):
        read = blocks_ref[n, 2]
        prior = jnp.int32(-1)
        for m in range(n):
            prior = jnp.where(read == m, newest[m], prior)
            newest[m] = jnp.where(read == m, n, newest[m])
        chain[0, n] = prior
    for m in range(count):
        chain[1, m] = newest[m]
    segv[...] = jnp.zeros_like(segv)
    segk[...] = jnp.zeros_like(segk)

    x_load.wait()
    xt[...] = xv[...].T

    @pl.when(first)
    def _():
        wo_load.wait()
        set_cot(cotfirst, dot(up_ref[...], wo_own[...]))

    pl.semaphore_wait(barrier, 2 * count)

    wo_push = remote(wo_ref, wo_next, ws, wr, (after, c))

    @pl.when(jnp.logical_not(first))
    def _():
        wo_push.start()

    def first_copy(d):
        h = to(d)
        return remote(cotfirst.at[h], cotin.at[c], fs.at[d], cr.at[d], (s, h))

    def cot_copy(d):
        h = to(d)
        return remote(cotsend.at[h], cotin.at[c], cs.at[d], cr.at[d], (before, h))

    def cot_arrival(d):
        n = source(d)
        return remote(cotsend.at[n], cotin.at[n], cs.at[d], cr.at[d], (s, n))

    def p_copy(h):
        return remote(psend.at[h], pin.at[c], ps.at[h], pr.at[c], (s, h))

    def p_arrival(h):
        return remote(psend.at[h], pin.at[h], ps.at[h], pr.at[h], (s, h))


    def project(i, carry):
        k = chunk_at(i)
        span = pl.ds(k * per_chunk, per_chunk)
        wi_load(k).wait()
        rows = wi[span].reshape(per_chunk * 4 * HD, width)
        psend[span] = dot(rows, xt[...]).astype(BF16).reshape(per_chunk, 4 * HD, BLOCK)
        for j in range(per_chunk):
            h = k * per_chunk + j

            @pl.when(h != c)
            def _(h=h):
                p_copy(h).start()

        return carry

    @pl.when(second)
    def _():
        pl.semaphore_wait(go, 1)

    lax.fori_loop(0, CHUNKS, project, 0)
    pin[c] = psend[c]

    @pl.when(first)
    def _():
        for d in far:
            first_copy(d).start()
        cotin[c] = cotfirst[c]
        upbuf[...] = up_ref[...]

    def x_copy(d):
        h = to(d)
        return remote(xv, xall.at[c], xs.at[d], xr.at[d], (s, h))

    def x_arrival(d):
        n = source(d)
        return remote(xv, xall.at[n], xs.at[d], xr.at[d], (s, n))

    def activate(d):
        n = source(d)
        if d:
            p_arrival(n).wait_recv()
        pre = pin[n].astype(F32)
        sigma = jax.nn.sigmoid(pre)
        act = (pre * sigma).astype(BF16)
        slopes = sigma * (1.0 + pre * (1.0 - sigma))
        gate[n] = act[:HD]
        value[n] = act[HD : 2 * HD]
        query[n] = act[2 * HD : 3 * HD]
        key[n] = act[3 * HD :]
        valuet[n] = act[HD : 2 * HD].astype(F32).T.astype(BF16)
        keyt[n] = act[3 * HD :].astype(F32).T.astype(BF16)
        fac[n, 0] = slopes[:HD]
        fac[n, 1] = slopes[2 * HD : 3 * HD]
        fac[n, 2] = slopes[HD : 2 * HD]
        fac[n, 3] = slopes[3 * HD :]

    for d in near:
        activate(d)

    @pl.when(first)
    def _():
        pl.semaphore_signal(go, inc=1, device_id=(before, c), device_id_type=MESH)

    @pl.when(jnp.logical_not(late))
    def _():
        for d in far:
            x_copy(d).start()

    xall[c] = xv[...]
    scale = HD ** (-0.5)
    gain = jnp.broadcast_to(gain_ref[c], (BLOCK, HD)).T
    apart = lax.broadcasted_iota(jnp.int32, (BLOCK, BLOCK), 0) - lax.broadcasted_iota(jnp.int32, (BLOCK, BLOCK), 1)

    def slots(n):
        return [blocks_ref[n, t] for t in range(3)]

    def attend(n, carry):
        listed = slots(n)
        at = [jnp.maximum(b, 0) for b in listed]
        scores = dot(jnp.concatenate([keyt[m] for m in at], axis=0), query[n]) * scale
        rank = row_ref[n].astype(F32)
        allowed = jnp.concatenate(
            [
                (apart <= (n - b) * BLOCK) & (col[m] == jnp.where(b >= 0, rank, -1.0))
                for b, m in zip(listed, at)
            ],
            axis=0,
        )
        sigma = jax.nn.sigmoid(scores)
        now = jnp.where(allowed, scores * sigma, 0.0).astype(BF16)
        weight[n] = now
        slope[n] = (jnp.where(allowed, sigma * (1.0 + scores * (1.0 - sigma)), 0.0) * scale).astype(BF16)
        attended = dot(jnp.concatenate([value[m] for m in at], axis=1), now)
        inv_rms = lax.rsqrt(jnp.sum(attended * attended, axis=0, keepdims=True) * (1.0 / HD) + 1.0)
        norm = attended * inv_rms
        normed[n] = norm
        ahead[n] = inv_rms * gain * gate[n].astype(F32)
        opening = gain * norm * fac[n, 0]
        fac[n, 0] = opening
        open_send[n] = opening.astype(BF16)
        return carry

    lax.fori_loop(0, count, attend, 0, unroll=4)

    def back_copy(src, landing, send, recv, d):
        n = source(d)
        return remote(src.at[n], landing.at[c], send.at[d], recv.at[d], (s, n))

    def query_copy(d):
        n = source(d)
        return remote(gpa.at[n, pl.ds(HD, HD)], gain_a.at[c], as_.at[d], ar.at[d], (s, n))

    def query_arrival(d):
        h = to(d)
        return remote(gpa.at[h, pl.ds(HD, HD)], gain_a.at[h], as_.at[d], ar.at[d], (s, h))

    def back_arrival(src, landing, send, recv, d):
        h = to(d)
        return remote(src.at[h], landing.at[h], send.at[d], recv.at[d], (s, h))

    for d in far:
        back_copy(open_send, open_all, gs_, gr, d).start()
    open_all[c] = open_send[c]

    def head(d):
        n = source(d)
        at = [jnp.maximum(b, 0) for b in slots(n)]
        cot_n = cotin[n].astype(F32)
        norm = normed[n]
        steep = cot_n * ahead[n]
        mean = jnp.sum(steep * norm, axis=0, keepdims=True) * (1.0 / HD)
        ga = (steep - norm * mean).astype(BF16)
        gw = dot(jnp.concatenate([valuet[m] for m in at], axis=0), ga)
        gs = (gw * slope[n].astype(F32)).astype(BF16)
        gq = dot(jnp.concatenate([key[m] for m in at], axis=1), gs)
        gpa[n, :HD] = (cot_n * fac[n, 0]).astype(BF16)
        gpa[n, HD:] = (gq * fac[n, 1]).astype(BF16)
        gvt[n] = ntdot(ga, weight[n])
        gkt[n] = ntdot(query[n], gs)

    group = 2
    for g in range(0, count, group):
        for d in near[g : g + group]:
            if d:
                cot_arrival(d).wait_recv()
            else:

                @pl.when(jnp.logical_not(first))
                def _(d=d):
                    cot_arrival(d).wait_recv()

        for d in near[g : g + group]:
            head(d)
        for d in near[g : g + group]:
            if d:
                query_copy(d).start()
    gain_a[c] = gpa[c, HD:]

    def seg_step(n, carry):
        prior = chain[0, n]
        back = jnp.maximum(prior, 0)
        keep = (prior >= 0).astype(F32)
        segv[n] = segv[back] * keep + gvt[n, :, 2 * BLOCK :]
        segk[n] = segk[back] * keep + gkt[n, :, 2 * BLOCK :]
        return carry

    lax.fori_loop(0, count, seg_step, 0, unroll=2)

    def finalise(d):
        m = source(d)
        later = lax.rem(m + 1, count)
        newest = chain[1, m]
        last = jnp.maximum(newest, 0)
        has = (newest >= 0).astype(F32)
        gv = gvt[m, :, :BLOCK] + gvt[later, :, BLOCK : 2 * BLOCK] + segv[last] * has
        gk = gkt[m, :, :BLOCK] + gkt[later, :, BLOCK : 2 * BLOCK] + segk[last] * has
        gpb[m, :HD] = (gv * fac[m, 2]).astype(BF16)
        gpb[m, HD:] = (gk * fac[m, 3]).astype(BF16)

    for d in far:
        finalise(d)
        back_copy(gpb, gain_b, bs, br, d).start()
    finalise(0)
    gain_b[c] = gpb[c]

    norm_factor = float(count * BLOCK) ** (-0.5)

    def weight_grad():
        for d in far[::-1]:
            x_arrival(d).wait_recv()
        whole = xall[...].reshape(count * BLOCK, width)
        for src, base in ((gpa, 0), (gpb, HD)):
            part = dot(jnp.concatenate([src[n] for n in range(count)], axis=1), whole) * norm_factor
            dw_ref[base : base + HD] = part[:HD]
            dw_ref[base + 2 * HD : base + 3 * HD] = part[HD:]

    def half_weights(parts, span):
        return jnp.concatenate([wi[h, p, :, span] for h in range(count) for p in parts], axis=0)

    own_push = remote(cotsend, cotown, os_, or_, (before, c))

    for d in near[1:]:
        back_arrival(open_send, open_all, gs_, gr, d).wait_recv()

    @pl.when(jnp.logical_not(first))
    def _():
        remote(sgsend, upbuf, us, ur, (s, c)).wait_recv()
        remote(cotsend, cotown, os_, or_, (s, c)).wait_recv()
        wo_push.wait_send()

    @pl.when(first)
    def _():
        cotown[...] = cotfirst[...]

    opened = (cotown[...].astype(F32) * open_all[...].astype(F32)).astype(BF16).reshape(count * HD, BLOCK)
    acc[...] = upbuf[...].astype(F32) + tdot(opened, half_weights((0,), slice(None)))
    for d in near[1:]:
        query_arrival(d).wait_recv()
    acc[...] += tdot(gain_a[...].reshape(count * HD, BLOCK), half_weights((2,), slice(None)))

    @pl.when(s == 0)
    def _():
        weight_grad()

    @pl.when(s > 0)
    def _():
        remote(wo_ref, wo_next, ws, wr, (s, c)).wait_recv()

    for d in near[1:]:
        back_arrival(gpb, gain_b, bs, br, d).wait_recv()
    left = gain_b[...].reshape(count * BLOCK, BLOCK)
    cols = width // CHUNKS
    for i in range(CHUNKS):
        span = slice(i * cols, (i + 1) * cols)
        part = (acc[:, span] + tdot(left, half_weights((1, 3), span))).astype(BF16)
        sgsend[:, span] = part
        sg_ref[:, span] = part

    up_push = remote(sgsend, upbuf, us, ur, (before, c))

    @pl.when(s > 0)
    def _():
        for dy in spiral:
            k = lax.rem(cy + dy, side)
            cols = pl.ds(pl.multiple_of(k * side * HD, side * HD), side * HD)
            part = dot(sgsend[...], wo_next[:, cols])
            cotsend[pl.ds(k * side, side)] = part.T.astype(BF16).reshape(side, HD, BLOCK)
            for dz in spiral:
                cot_copy(dy * side + dz).start()
        up_push.start()
        own_push.start()

    @pl.when(second)
    def _():
        pl.semaphore_signal(go, inc=1, device_id=(after, c), device_id_type=MESH)

    @pl.when(first)
    def _():
        pl.semaphore_wait(go, 1)

    @pl.when(late)
    def _():
        for d in far:
            x_copy(d).start()

    @pl.when(s > 0)
    def _():
        weight_grad()

    @pl.when(first)
    def _():
        for d in far:
            first_copy(d).wait_send()

    for d in far:
        p_copy(to(d)).wait_send()
        query_copy(d).wait_send()
        back_copy(open_send, open_all, gs_, gr, d).wait_send()
        back_copy(gpb, gain_b, bs, br, d).wait_send()
        x_copy(d).wait_send()

    @pl.when(s > 0)
    def _():
        for d in far + [0]:
            cot_copy(d).wait_send()
        up_push.wait_send()
        own_push.wait_send()


def per_device(key_blocks, ranker, section_inputs, output_grad, input_proj, output_proj, norm_gain):
    count = lax.axis_size("ctx")
    x = section_inputs[0, 0]
    width = x.shape[1]
    blocks = key_blocks[0]
    gain = norm_gain[0].reshape(count, 1, HD)
    ranks = ranker[0].reshape(count, 1, BLOCK)
    vmem = pl.BlockSpec(memory_space=pltpu.VMEM)
    smem = pl.BlockSpec(memory_space=pltpu.SMEM)
    hbm = pl.BlockSpec(memory_space=pl.ANY)
    dma = pltpu.SemaphoreType.DMA
    full = 3 * BLOCK

    def half(*shape):
        return pltpu.VMEM(shape, BF16)

    def single(*shape):
        return pltpu.VMEM(shape, F32)

    sg, dw = pl.pallas_call(
        kernel,
        out_shape=(
            jax.ShapeDtypeStruct((BLOCK, width), BF16),
            jax.ShapeDtypeStruct((4 * HD, width), F32),
        ),
        in_specs=[smem, vmem, vmem, vmem, hbm, hbm, hbm],
        out_specs=(vmem, vmem),
        scratch_shapes=[
            half(BLOCK, width),
            half(width, BLOCK),
            half(count, 4, HD, width),
            half(width, width),
            half(width, width),
            half(count, 4 * HD, BLOCK),
            half(count, 4 * HD, BLOCK),
            half(count, BLOCK, width),
            half(count, HD, BLOCK),
            half(count, HD, BLOCK),
            half(count, HD, BLOCK),
            half(count, HD, BLOCK),
            half(count, BLOCK, HD),
            half(count, BLOCK, HD),
            half(count, full, BLOCK),
            half(count, full, BLOCK),
            single(count, HD, BLOCK),
            single(count, HD, BLOCK),
            single(count, 4, HD, BLOCK),
            single(count, BLOCK, BLOCK),
            half(BLOCK, width),
            half(BLOCK, width),
            half(count, HD, BLOCK),
            half(count, HD, BLOCK),
            half(count, HD, BLOCK),
            half(count, HD, BLOCK),
            half(count, HD, BLOCK),
            half(count, HD, BLOCK),
            half(count, 2 * HD, BLOCK),
            half(count, 2 * HD, BLOCK),
            half(count, HD, BLOCK),
            half(count, 2 * HD, BLOCK),
            single(count, HD, full),
            single(count, HD, full),
            single(count, HD, BLOCK),
            single(count, HD, BLOCK),
            single(BLOCK, width),
            dma,
            dma((CHUNKS,)),
            dma,
        ]
        + [dma((count,)) for _ in range(11)]
        + [dma for _ in range(6)]
        + [dma((count,)) for _ in range(2)]
        + [pltpu.SemaphoreType.REGULAR, pltpu.SMEM((2, count), jnp.int32)],
        compiler_params=pltpu.CompilerParams(
            collective_id=0, has_side_effects=True, vmem_limit_bytes=58 * 1024 * 1024
        ),
        cost_estimate=pl.CostEstimate(flops=5 * 10**9, bytes_accessed=20 * 10**6, transcendentals=0),
    )(
        blocks, output_grad[0], gain, ranks,
        x, input_proj[0].reshape(count, 4, HD, width), output_proj[0],
    )
    return sg[None, None], dw[None]


def solution(mesh):
    placed = (
        P(),
        P(),
        P("pipe", None, "ctx", None),
        P(None, "ctx", None),
        P("pipe", None, None),
        P("pipe", None, None),
        P("pipe", None),
    )
    return jax.shard_map(
        per_device,
        mesh=mesh,
        in_specs=placed,
        out_specs=(P("pipe", None, "ctx", None), P("pipe", "ctx", None)),
        check_vma=False,
    )
```
